128 devices in a mesh: rep: 16 (over z_lo, x, core), fsdp: 8 (over z_hi, y).
Axes of the slice: x: 4, y: 4, z: 4 (z_hi: 2, z_lo: 2; z = z_hi * 2 + z_lo), core: 2. Of those that a mesh axis runs over, the one named last changes fastest.
Arguments:
- tokens: bfloat16 [16, 4096, 4096], P('rep', 'fsdp'), may hold values from -6 to 6
- gain: bfloat16 [16, 4096], P('rep', 'fsdp'), may hold values from 0.3984375 to 2
- weight: bfloat16 [16, 4096, 1024], P('rep', 'fsdp'), may hold values from -0.09375 to 0.09375
- w_first: float32 [16, 4096, 1024], P('rep', 'fsdp'), may hold values from -120 to 120
- w_second: float32 [16, 4096, 1024], P('rep', 'fsdp'), may hold values from 10 to 1000
- g_first: float32 [16, 4096], P('rep', 'fsdp'), may hold values from -60 to 60
- g_second: float32 [16, 4096], P('rep', 'fsdp'), may hold values from 10 to 1000
- cotangent: bfloat16 [16, 4096, 1024], P('rep', 'fsdp'), may hold values from -6 to 6
- exponent: int32 [4], replicated, may hold values from 0 to 2
Outputs:
- values: bfloat16 [16, 4096, 1024], P('rep', 'fsdp')
- input_grad: bfloat16 [16, 4096, 4096], P('rep', 'fsdp')
- new_weight: bfloat16 [16, 4096, 1024], P('rep', 'fsdp')
- new_wfirst: float32 [16, 4096, 1024], P('rep', 'fsdp')
- new_wsecond: float32 [16, 4096, 1024], P('rep', 'fsdp')
- new_gain: bfloat16 [16, 4096], P('rep', 'fsdp')
- new_gfirst: float32 [16, 4096], P('rep', 'fsdp')
- new_gsecond: float32 [16, 4096], P('rep', 'fsdp')
The draws below stay inside these ranges and needn't reach their ends.
Inputs may be any that keep to these rules, and one draw needn't show every extreme that they name: `exponent`: each round's k is the same for all replicas.
All inputs are finite; a program needn't handle non-finite values.
Results may differ from the reference program's by a relative error of at most 0.0068.
Values may be sent and summed in bfloat16 or wider, within the bound.
A program may use at most 128 MiB of HBM per device.

```python
import math
import jax
import jax.numpy as jnp
from jax import lax

D = 4096
KVW = 1024
STEP = 10
ROUNDS = 4
TOKENS = 4096
N_REP = 16


def with_ends(values, rng, smallest, high):
    extent = values.shape
    place = [jax.random.randint(jax.random.fold_in(rng, axis), (), 0, extent[axis]) for axis in range(len(extent))]
    values = values.at[tuple(place)].set(smallest)
    longest = extent.index(max(extent))
    place[longest] = (place[longest] + 1) % extent[longest]
    return values.at[tuple(place)].set(high)


def level_of(stream_key, extent, shards, low, high):
    level = 1.0
    for dim, parts in shards:
        draws = jax.random.uniform(jax.random.fold_in(jax.random.fold_in(stream_key, 6), dim), (parts,), jnp.float32, low / len(shards), high / len(shards))
        level = level * jnp.repeat(jnp.exp(draws), extent[dim] // parts).reshape((-1,) + (1,) * (len(extent) - 1 - dim))
    return level


def bell_draw(stream_key, dims, width, limit, shards=(), kind=jnp.bfloat16):
    level = level_of(stream_key, dims, shards, -0.22, 0.18) if shards else 1.0
    drawn = jax.random.normal(stream_key, dims, jnp.float32) * width * level
    return jnp.minimum(jnp.maximum(drawn, -limit), limit).astype(kind)


def setup_inputs(seed: int = 0) -> dict:
    key_of = jax.random.split(jax.random.key(seed), 10)
    tokens = bell_draw(key_of[0], (N_REP, TOKENS, D), 1.0, 6.0, ((0, 16), (1, 8)))
    gain = jnp.clip(0.3984375 + 1.6015625 * jax.random.uniform(key_of[1], (N_REP, D), jnp.float32) ** level_of(key_of[1], (N_REP, D), ((0, 16), (1, 8)), -0.2, 0.2), 0.3984375, 2.0).astype(jnp.bfloat16)
    weight = bell_draw(key_of[2], (N_REP, D, KVW), D ** -0.5, 0.09375, ((0, 16), (1, 8)))
    w_first = bell_draw(key_of[3], (N_REP, D, KVW), 20.0, 120.0, ((0, 16), (1, 8)), jnp.float32)
    w_second = jnp.clip(jnp.exp(math.log(1000.0) - 4.6051702 * jax.random.uniform(key_of[4], (N_REP, D, KVW), jnp.float32) ** level_of(key_of[4], (N_REP, D, KVW), ((0, 16), (1, 8)), -0.2, 0.2)), 10.0, 1000.0)
    g_first = bell_draw(key_of[5], (N_REP, D), 10.0, 60.0, ((0, 16), (1, 8)), jnp.float32)
    g_second = jnp.clip(jnp.exp(math.log(1000.0) - 4.6051702 * jax.random.uniform(key_of[6], (N_REP, D), jnp.float32) ** level_of(key_of[6], (N_REP, D), ((0, 16), (1, 8)), -0.2, 0.2)), 10.0, 1000.0)
    cotangent = bell_draw(key_of[7], (N_REP, TOKENS, KVW), 1.0, 6.0, ((0, 16), (1, 8)))
    exponent = with_ends(jax.random.randint(key_of[8], (ROUNDS,), 0, 3), jax.random.fold_in(key_of[8], 1), 0, 2).astype(jnp.int32)
    return dict(tokens=tokens, gain=gain, weight=weight, w_first=w_first, w_second=w_second, g_first=g_first, g_second=g_second, cotangent=cotangent, exponent=exponent)


def adam(param, grad, first, second):
    new_first = 0.9 * first + 0.1 * grad
    new_second = 0.95 * second + 0.05 * grad * grad
    fix_first = 1.0 - 0.9 ** STEP
    fix_second = 1.0 - 0.95 ** STEP
    pf = param.astype(jnp.float32)
    update = new_first / fix_first / (jnp.sqrt(new_second / fix_second) + 1e-08) + 0.1 * pf
    return ((pf - 0.003 * update).astype(jnp.bfloat16), new_first, new_second)

def replica(tokens, gain, weight, w_first, w_second, g_first, g_second, cotangent):
    xf = tokens.astype(jnp.float32)
    rstd = lax.rsqrt(lax.optimization_barrier(jnp.mean(xf * xf, axis=1, keepdims=True)) + 1e-05)
    gfull = gain.astype(jnp.float32)
    normed = (xf * rstd * gfull[None, :]).astype(jnp.bfloat16)
    values = jnp.dot(normed, weight, preferred_element_type=jnp.float32).astype(jnp.bfloat16)
    dnorm = jnp.dot(cotangent, weight.T, preferred_element_type=jnp.float32)
    gain_grad = lax.optimization_barrier(jnp.sum(dnorm * xf * rstd, axis=0))
    scaled = dnorm * gfull[None, :]
    inner = lax.optimization_barrier(jnp.mean(scaled * xf, axis=1, keepdims=True))
    input_grad = (rstd * (scaled - xf * rstd * rstd * inner)).astype(jnp.bfloat16)
    weight_grad = jnp.dot(normed.T, cotangent, preferred_element_type=jnp.float32)
    w_step, nwf, nws = adam(weight, weight_grad, w_first, w_second)
    g_step, ngf, ngs = adam(gain, gain_grad, g_first, g_second)
    return (values, input_grad, w_step, nwf, nws, g_step, ngf, ngs)

def reference(tokens, gain, weight, w_first, w_second, g_first, g_second, cotangent, exponent):
    outs = jax.vmap(replica)(tokens, gain, weight, w_first, w_second, g_first, g_second, cotangent)
    values, input_grad, w_step, nwf, nws, g_step, ngf, ngs = outs
    indices = jnp.arange(N_REP, dtype=jnp.int32)
    for level in range(ROUNDS):
        partner = jnp.bitwise_xor(indices, jnp.left_shift(jnp.int32(1), exponent[level]))
        w_step = ((w_step.astype(jnp.float32) + w_step[partner].astype(jnp.float32)) * 0.5).astype(jnp.bfloat16)
        g_step = ((g_step.astype(jnp.float32) + g_step[partner].astype(jnp.float32)) * 0.5).astype(jnp.bfloat16)
    return (values, input_grad, w_step, nwf, nws, g_step, ngf, ngs)
```

```python
import functools

import jax
import jax.numpy as jnp
from jax import lax
from jax.experimental import pallas as pl
from jax.experimental.pallas import tpu as pltpu
from jax.sharding import PartitionSpec as P

STEP = 10
ROUNDS = 4
T = 512
B = 512
D = 4096
KV = 1024
NS = 160
NL = 48
GP = 128
MESH = pl.DeviceIdType.MESH
F32 = jnp.float32
BF16 = jnp.bfloat16


def adam(param, grad, first, second):
    new_first = 0.9 * first + 0.1 * grad
    new_second = 0.95 * second + 0.05 * grad * grad
    fix_first = 1.0 - 0.9**STEP
    fix_second = 1.0 - 0.95**STEP
    update = new_first / fix_first / (jnp.sqrt(new_second / fix_second) + 1e-08) + 0.1 * param
    return (param - 0.003 * update).astype(BF16), new_first, new_second


def averaged(parts, exponents):
    for e in exponents:
        mixed = []
        for j in range(8):
            partner = jnp.where(e == 0, parts[j ^ 1], jnp.where(e == 1, parts[j ^ 2], parts[j ^ 4]))
            mixed.append(((parts[j] + partner) * 0.5).astype(BF16).astype(F32))
        parts = mixed
    return parts


def kernel(
    x_hbm, gain_ref, w_hbm, m_hbm, v_hbm, gm_ref, gv_ref, cot_hbm, exp_ref,
    val_hbm, ig_hbm, nw_hbm, nm_hbm, nv_hbm, ng_ref, ngm_ref, ngv_ref,
    xb, nrm, nt, ntp, wb, cot, cotp, acc, own, vout, rstd, slope,
    gb, ggs, ggr, gxs, gxr,
    sd, sr, sl, dr, dl, rr, rl, m_v, v_v, gs, gr, gt, wn,
    ssem, rsem, lsem,
):
    rep = lax.axis_index("rep")
    f = lax.axis_index("fsdp")
    h, y = f // 4, f % 4
    zlo, rank = rep // 8, rep % 8
    bits = (rank % 2, (rank // 2) % 2, rank // 4)

    def shard(dh, dy):
        return (1 - h if dh else h) * 4 + (y + dy) % 4

    def peer(dh, dy):
        return (rep, shard(dh, dy))

    def mate_rank(j):
        return sum((1 - b if (j >> i) & 1 else b) * (1 << i) for i, b in enumerate(bits))

    def mate(j):
        return (zlo * 8 + mate_rank(j), f)

    right, left, across = peer(0, 1), peer(0, 3), peer(1, 0)

    sent, kept = [], []

    def send(src, dst, device):
        i = len(sent)
        copy = pltpu.make_async_remote_copy(
            src_ref=src, dst_ref=dst, send_sem=ssem.at[i], recv_sem=rsem.at[i],
            device_id=device, device_id_type=MESH,
        )
        copy.start()
        sent.append(copy)
        return copy

    def move(src, dst):
        copy = pltpu.make_async_copy(src, dst, lsem.at[len(kept)])
        copy.start()
        kept.append(copy)
        return copy

    def rows(start, size):
        return pl.ds(start, size)

    barrier = pltpu.get_barrier_semaphore()
    others = [peer(i // 4, i % 4) for i in range(1, 8)] + [mate(j) for j in range(1, 8)]
    for device in others:
        pl.semaphore_signal(barrier, inc=1, device_id=device, device_id_type=MESH)
    pl.semaphore_wait(barrier, len(others))

    def send_wz(k):
        return send(w_hbm.at[0, rows(128 * k, 128)], wb.at[4, rows(128 * k, 128)], across)

    wz = [send_wz(0), send_wz(1)]
    a1r = [send(w_hbm.at[0, rows(0, 256)], wb.at[3, rows(0, 256)], right)]
    a1l = [send(w_hbm.at[0, rows(256, 256)], wb.at[1, rows(256, 256)], left)]
    a1r.append(send(w_hbm.at[0, rows(256, 256)], wb.at[3, rows(256, 256)], right))
    a1l.append(send(w_hbm.at[0, rows(0, 256)], wb.at[1, rows(0, 256)], left))

    gb[0] = jnp.broadcast_to(gain_ref[...].astype(F32), (8, B))
    gains = [
        send(gb.at[0], gb.at[4 * (i // 4) + (4 - i % 4) % 4], peer(i // 4, i % 4))
        for i in range(1, 8)
    ]

    def columns(b):
        return pl.ds(pl.multiple_of(shard(b // 4, b % 4) * B, B), B)

    x_in = [move(x_hbm.at[0, :, columns(b)], xb.at[b]) for b in range(8)]
    cot_in = move(cot_hbm.at[0], cot)
    w_in = move(w_hbm.at[0], wb.at[0])
    m_in = move(m_hbm.at[0], m_v)
    v_in = move(v_hbm.at[0], v_v)
    for copy in x_in:
        copy.wait()

    @pl.loop(0, T // 64)
    def _(i):
        r = pl.ds(pl.multiple_of(i * 64, 64), 64)
        total = jnp.zeros((64, B), F32)
        for b in range(8):
            xf = xb[b, r, :].astype(F32)
            total += xf * xf
        mean = jnp.sum(total, axis=1, keepdims=True) * (1.0 / D)
        rstd[r, :] = jnp.broadcast_to(lax.rsqrt(mean + 1e-05), (64, 128))

    for copy in gains:
        copy.wait_recv()

    def normalise(first, last):
        @pl.loop(first, last)
        def _(b):
            g = gb[b, 0:1, :]

            @pl.loop(0, T // 128)
            def _(i):
                r = pl.ds(pl.multiple_of(i * 128, 128), 128)
                tile = (xb[b, r, :].astype(F32) * rstd[r, 0:1] * g).astype(BF16)
                nrm[b, r, :] = tile
                nt[b, :, r] = tile.T

    def forward_wz(k):
        wz[k].wait_recv()
        piece = rows(128 * k, 128)
        return (
            send(wb.at[4, piece], wb.at[7, piece], right),
            send(wb.at[4, piece], wb.at[5, piece], left),
        )

    def add_values(b, first=False):
        @pl.loop(0, KV // 256)
        def _(n):
            c = pl.ds(pl.multiple_of(n * 256, 256), 256)
            part = jnp.dot(nrm[b], wb[b, :, c], preferred_element_type=F32)
            acc[:, c] = part if first else acc[:, c] + part

    a2 = [forward_wz(0)]
    wz.append(send_wz(2))
    normalise(4, 8)
    a2.append(forward_wz(1))
    wz.append(send_wz(3))
    normalise(0, 4)
    w_in.wait()
    add_values(0, True)
    a2.append(forward_wz(2))
    cot_in.wait()
    cot_z = send(cot, cotp, across)
    a2.append(forward_wz(3))

    def send_nt(dy, pair):
        r = rows(256 * pair, 256)
        return send(nt.at[4 + dy, r], ntp.at[dy, r], across)

    nt2 = [send_nt(2, 0), send_nt(2, 1)]

    a1r[0].wait_recv()
    a3r = send(wb.at[3, rows(0, 256)], wb.at[2, rows(0, 256)], right)
    a1l[0].wait_recv()
    a3l = send(wb.at[1, rows(256, 256)], wb.at[2, rows(256, 256)], left)
    a1r[1].wait_recv()
    a1l[1].wait_recv()
    add_values(1)
    add_values(3)
    add_values(4)
    for pair in a2:
        pair[0].wait_recv()
        pair[1].wait_recv()
    a4r = send(wb.at[7, rows(0, 192)], wb.at[6, rows(0, 192)], right)
    a4l = send(wb.at[5, rows(320, 192)], wb.at[6, rows(320, 192)], left)
    add_values(5)
    add_values(7)
    cot_z.wait_recv()
    nt1, nt3, nt0 = [send_nt(1, 0)], [send_nt(3, 0)], []
    a3r.wait_recv()
    a3l.wait_recv()
    a4z = send(wb.at[2, rows(192, 128)], wb.at[6, rows(192, 128)], across)

    def gradient(dy, pair, write):
        r = rows(256 * pair, 256)

        @pl.loop(0, KV // 256)
        def _(n):
            c = pl.ds(pl.multiple_of(n * 256, 256), 256)
            part = jnp.dot(nt[dy, r, :], cot[:, c], preferred_element_type=F32)
            part += jnp.dot(ntp[dy, r, :], cotp[:, c], preferred_element_type=F32)
            write(c, part)

    d2 = []
    for pair in range(2):
        nt2[pair].wait_recv()

        def write(c, part, pair=pair):
            sd[rows(256 * pair, 256), c] = part.astype(BF16)

        gradient(2, pair, write)
        there = rows(128 * pair, 128)
        d2.append(send(sd.at[rows(256 * pair, 128)], dr.at[there], right))
        d2.append(send(sd.at[rows(256 * pair + 128, 128)], dl.at[there], left))
    add_values(2)

    def pass_on(pair):
        (nt1[pair]).wait_recv()
        d2[2 * pair].wait_recv()
        there = rows(128 * pair, 128)
        top, low = rows(256 * pair, 128), rows(256 * pair + 128, 128)

        def write_right(c, part):
            sr[top, c] = (part[:128] + dr[there, c].astype(F32)).astype(BF16)
            sr[low, c] = part[128:].astype(BF16)

        gradient(1, pair, write_right)
        rights = [send(sr.at[r], rr.at[r], right) for r in (top, low)]
        (nt3[pair]).wait_recv()
        d2[2 * pair + 1].wait_recv()

        def write_left(c, part):
            sl[top, c] = part[:128].astype(BF16)
            sl[low, c] = (part[128:] + dl[there, c].astype(F32)).astype(BF16)

        gradient(3, pair, write_left)
        lefts = [send(sl.at[r], rl.at[r], left) for r in (top, low)]
        return list(zip(rights, lefts, strict=True))

    nt1.append(send_nt(1, 1))
    nt3.append(send_nt(3, 1))
    for copy in (a4r, a4l, a4z):
        copy.wait_recv()
    add_values(6)
    arriving = pass_on(0)
    nt0 += [send_nt(0, 0), send_nt(0, 1)]

    @pl.loop(0, T // 64)
    def _(i):
        r = pl.ds(pl.multiple_of(i * 64, 64), 64)
        total = acc[r, :]
        vout[r, :] = total.astype(BF16)
        inner = jnp.sum(total * cot[r, :].astype(F32), axis=1, keepdims=True) * (1.0 / D)
        slope[r, :] = inner * rstd[r, :]

    move(vout, val_hbm.at[0])

    def backward(first, last):
        @pl.loop(first, last)
        def _(b):
            for n in range(B // 256):
                c = pl.ds(n * 256, 256)
                g = gb[b, 0:1, c]
                dn = lax.dot_general(
                    cot[...], wb[b, c, :], (((1,), (1,)), ((), ())), preferred_element_type=F32
                )
                xf = xb[b, :, c].astype(F32)
                rs = rstd[:, 0:1]
                xb[b, :, c] = (rs * (dn * g - xf * slope[:, 0:1])).astype(BF16)
                share = dn * xf * rs
                ggs[b, :, c] = jnp.sum(share.reshape(T // 8, 8, 256), axis=0)

        for b in range(first, last):
            move(xb.at[b], ig_hbm.at[0, :, columns(b)])

    backward(0, 4)
    arriving += pass_on(1)
    backward(4, 8)
    gg = [
        send(ggs.at[i], ggr.at[4 * (i // 4) + (4 - i % 4) % 4], peer(i // 4, i % 4))
        for i in range(1, 8)
    ]

    exponents = [exp_ref[i] for i in range(ROUNDS)]
    m_in.wait()
    v_in.wait()
    n_pieces = B // GP
    out1, out2 = [], []

    def own_gradient(pair):
        nt0[pair].wait_recv()

        def write(c, part):
            own[rows(256 * pair, 256), c] = part

        gradient(0, pair, write)

    def step(p):
        r = rows(GP * p, GP)
        for copy in arriving[p]:
            copy.wait_recv()
        for e in range(8):
            c = pl.ds(128 * e, 128)
            grad = own[r, c] + rr[r, c].astype(F32) + rl[r, c].astype(F32)
            stepped, m_v[r, c], v_v[r, c] = adam(wb[0, r, c].astype(F32), grad, m_v[r, c], v_v[r, c])
            gs[p, e] = stepped
        out1.append([send(gs.at[p, mate_rank(j)], gr.at[p, j], mate(j)) for j in range(1, 8)])
        move(m_v.at[r], nm_hbm.at[0, r])
        move(v_v.at[r], nv_hbm.at[0, r])

    mine = pl.ds(pl.multiple_of(rank * 128, 128), 128)

    def mix(p):
        r = rows(GP * p, GP)
        for copy in out1[p]:
            copy.wait_recv()

        @pl.loop(0, GP // 32)
        def _(i):
            q = pl.ds(pl.multiple_of(i * 32, 32), 32)
            parts = [gs[p, rank, q, :].astype(F32)]
            parts += [gr[p, j, q, :].astype(F32) for j in range(1, 8)]
            parts = averaged(parts, exponents)
            for j in range(8):
                gt[p, j, q, :] = parts[j].astype(BF16)

        out2.append([send(gt.at[p, j], wn.at[r, mine], mate(j)) for j in range(1, 8)])
        wn[r, mine] = gt[p, 0]

    def finish(p):
        r = rows(GP * p, GP)
        for copy in out2[p]:
            copy.wait_recv()
        move(wn.at[r], nw_hbm.at[0, r])

    own_gradient(0)
    step(0)
    step(1)

    for copy in gg:
        copy.wait_recv()
    total = ggs[0]
    for i in range(1, 8):
        total += ggr[i]
    grad = jnp.sum(total, axis=0, keepdims=True)
    stepped, ngm_ref[...], ngv_ref[...] = adam(
        gain_ref[...].astype(F32), grad, gm_ref[...], gv_ref[...]
    )
    gxs[...] = jnp.broadcast_to(stepped.astype(F32), (8, B))
    gx = [send(gxs, gxr.at[j], mate(j)) for j in range(1, 8)]

    mix(0)
    own_gradient(1)
    step(2)
    mix(1)
    for copy in gx:
        copy.wait_recv()
    parts = averaged([gxs[...]] + [gxr[j] for j in range(1, 8)], exponents)
    ng_ref[...] = parts[0][0:1].astype(BF16)
    finish(0)
    step(3)
    mix(2)
    finish(1)
    mix(3)
    finish(2)
    finish(3)

    for copy in sent:
        copy.wait_send()
    for copy in kept[12:]:
        copy.wait()


def local(*args):
    any_space, vmem = pl.BlockSpec(memory_space=pl.ANY), pl.BlockSpec(memory_space=pltpu.VMEM)
    smem = pl.BlockSpec(memory_space=pltpu.SMEM)
    shapes = [
        ((1, T, KV), BF16), ((1, T, D), BF16), ((1, B, KV), BF16), ((1, B, KV), F32), ((1, B, KV), F32),
        ((1, B), BF16), ((1, B), F32), ((1, B), F32),
    ]
    scratch = [
        ((8, T, B), BF16), ((8, T, B), BF16), ((8, B, T), BF16), ((4, B, T), BF16),
        ((8, B, KV), BF16), ((T, KV), BF16), ((T, KV), BF16),
        ((T, KV), F32), ((B, KV), F32), ((T, KV), BF16), ((T, 128), F32), ((T, 128), F32),
        ((8, 8, B), F32), ((8, 8, B), F32), ((8, 8, B), F32), ((8, B), F32), ((8, 8, B), F32),
        ((B, KV), BF16), ((B, KV), BF16), ((B, KV), BF16), ((B // 2, KV), BF16), ((B // 2, KV), BF16),
        ((B, KV), BF16), ((B, KV), BF16), ((B, KV), F32), ((B, KV), F32),
        ((B // GP, 8, GP, 128), BF16), ((B // GP, 8, GP, 128), BF16), ((B // GP, 8, GP, 128), BF16), ((B, KV), BF16),
    ]
    return pl.pallas_call(
        kernel,
        out_shape=[jax.ShapeDtypeStruct(s, t) for s, t in shapes],
        in_specs=[any_space, vmem, any_space, any_space, any_space, vmem, vmem, any_space, smem],
        out_specs=[any_space] * 5 + [vmem] * 3,
        scratch_shapes=[pltpu.VMEM(s, t) for s, t in scratch]
        + [pltpu.SemaphoreType.DMA((NS,)), pltpu.SemaphoreType.DMA((NS,)), pltpu.SemaphoreType.DMA((NL,))],
        compiler_params=pltpu.CompilerParams(
            collective_id=0, has_side_effects=True, vmem_limit_bytes=60 << 20
        ),
        cost_estimate=pl.CostEstimate(flops=6 * T * D * KV, bytes_accessed=20 << 20, transcendentals=0),
        name="layer_step",
    )(*args)


def solution(mesh):
    split, vector = P("rep", "fsdp", None), P("rep", "fsdp")
    return jax.shard_map(
        local,
        mesh=mesh,
        in_specs=(split, vector, split, split, split, vector, vector, split, P()),
        out_specs=(split, split, split, split, split, vector, vector, vector),
        check_vma=False,
    )
```

```python
import functools

import jax
import jax.numpy as jnp
from jax import lax
from jax.experimental import pallas as pl
from jax.experimental.pallas import tpu as pltpu
from jax.sharding import PartitionSpec as P

STEP = 10
ROUNDS = 4
T = 512
B = 512
D = 4096
KV = 1024
NS = 160
NL = 48
PIECES = ((0, 128), (128, 128), (256, 128), (384, 64), (448, 64))
MESH = pl.DeviceIdType.MESH
F32 = jnp.float32
BF16 = jnp.bfloat16


def adam(param, grad, first, second):
    new_first = 0.9 * first + 0.1 * grad
    new_second = 0.95 * second + 0.05 * grad * grad
    fix_first = 1.0 - 0.9**STEP
    fix_second = 1.0 - 0.95**STEP
    update = new_first / fix_first / (jnp.sqrt(new_second / fix_second) + 1e-08) + 0.1 * param
    return (param - 0.003 * update).astype(BF16), new_first, new_second


def averaged(parts, exponents):
    for e in exponents:
        mixed = []
        for j in range(8):
            partner = jnp.where(e == 0, parts[j ^ 1], jnp.where(e == 1, parts[j ^ 2], parts[j ^ 4]))
            mixed.append(((parts[j] + partner) * 0.5).astype(BF16).astype(F32))
        parts = mixed
    return parts


def packed(row):
    return jnp.concatenate([row[:, 128 * i : 128 * (i + 1)] for i in range(4)] + [jnp.zeros((4, 128), F32)], axis=0)


def unpacked(tile):
    return jnp.concatenate([tile[i : i + 1] for i in range(4)], axis=1)


def kernel(
    x_hbm, gain_ref, w_hbm, m_hbm, v_hbm, gm_ref, gv_ref, cot_hbm, exp_ref,
    vout, xb, wn, m_v, v_v, gout,
    nrm, nt, ntp, wb, cot, cotp, acc, own, held, rstd, slope,
    gb, ggs, ggr, gxs, gxr,
    sd, sr, sl, dr, dl, rr, rl, gs, gr, gt,
    ssem, rsem, lsem,
):
    rep = lax.axis_index("rep")
    f = lax.axis_index("fsdp")
    h, y = f // 4, f % 4
    zlo, rank = rep // 8, rep % 8
    bits = (rank % 2, (rank // 2) % 2, rank // 4)

    def shard(dh, dy):
        return (1 - h if dh else h) * 4 + (y + dy) % 4

    def peer(dh, dy):
        return (rep, shard(dh, dy))

    def mate_rank(j):
        return sum((1 - b if (j >> i) & 1 else b) * (1 << i) for i, b in enumerate(bits))

    def mate(j):
        return (zlo * 8 + mate_rank(j), f)

    right, left, across = peer(0, 1), peer(0, 3), peer(1, 0)

    sent, kept = [], []

    def send(src, dst, device):
        i = len(sent)
        copy = pltpu.make_async_remote_copy(
            src_ref=src, dst_ref=dst, send_sem=ssem.at[i], recv_sem=rsem.at[i],
            device_id=device, device_id_type=MESH,
        )
        copy.start()
        sent.append(copy)
        return copy

    def move(src, dst):
        copy = pltpu.make_async_copy(src, dst, lsem.at[len(kept)])
        copy.start()
        kept.append(copy)
        return copy

    def rows(start, size):
        return pl.ds(start, size)

    barrier = pltpu.get_barrier_semaphore()
    others = [peer(i // 4, i % 4) for i in range(1, 8)] + [mate(j) for j in range(1, 8)]
    for device in others:
        pl.semaphore_signal(barrier, inc=1, device_id=device, device_id_type=MESH)
    pl.semaphore_wait(barrier, len(others))

    def back(i):
        return 4 * (i // 4) + (4 - i % 4) % 4

    gb[0] = packed(gain_ref[...].astype(F32))
    gains = [send(gb.at[0], gb.at[back(i)], peer(i // 4, i % 4)) for i in range(1, 8)]

    a1r, a1l, wz = [], [], []
    for k in range(2):
        for pieces, slot, half, device in ((a1r, 3, k, right), (a1l, 1, 1 - k, left)):
            r = rows(256 * half, 256)
            pieces.append(send(w_hbm.at[0, r], wb.at[slot, r], device))
        for q in (2 * k, 2 * k + 1):
            r = rows(128 * q, 128)
            wz.append(send(w_hbm.at[0, r], wb.at[4, r], across))
    cot_z = send(cot_hbm.at[0], cotp, across)

    def columns(b):
        return pl.ds(pl.multiple_of(shard(b // 4, b % 4) * B, B), B)

    x_in = [move(x_hbm.at[0, :, columns(b)], xb.at[b]) for b in range(8)]
    cot_in = move(cot_hbm.at[0], cot)
    w_in = move(w_hbm.at[0], wb.at[0])
    m_in = move(m_hbm.at[0], m_v)
    v_in = move(v_hbm.at[0], v_v)
    for copy in x_in:
        copy.wait()

    @pl.loop(0, T // 64)
    def _(i):
        r = pl.ds(pl.multiple_of(i * 64, 64), 64)
        total = jnp.zeros((64, B), F32)
        for b in range(8):
            xf = xb[b, r, :].astype(F32)
            total += xf * xf
        mean = jnp.sum(total, axis=1, keepdims=True) * (1.0 / D)
        rstd[r, :] = jnp.broadcast_to(lax.rsqrt(mean + 1e-05), (64, 128))

    for copy in gains:
        copy.wait_recv()

    def normalise(first, last):
        @pl.loop(first, last)
        def _(b):
            g = unpacked(gb[b])

            @pl.loop(0, T // 128)
            def _(i):
                r = pl.ds(pl.multiple_of(i * 128, 128), 128)
                tile = (xb[b, r, :].astype(F32) * rstd[r, 0:1] * g).astype(BF16)
                nrm[b, r, :] = tile
                nt[b, :, r] = tile.T

    def forward_wz(k):
        wz[k].wait_recv()
        piece = rows(128 * k, 128)
        return (
            send(wb.at[4, piece], wb.at[7, piece], right),
            send(wb.at[4, piece], wb.at[5, piece], left),
        )

    def add_values(b, first=False):
        @pl.loop(0, KV // 256)
        def _(n):
            c = pl.ds(pl.multiple_of(n * 256, 256), 256)
            part = jnp.dot(nrm[b], wb[b, :, c], preferred_element_type=F32)
            acc[:, c] = part if first else acc[:, c] + part

    def send_nt(dy, pair):
        r = rows(256 * pair, 256)
        return send(nt.at[4 + dy, r], ntp.at[dy, r], across)

    a2 = [forward_wz(0)]
    normalise(4, 8)
    a2.append(forward_wz(1))
    nts = {(dy, 0): send_nt(dy, 0) for dy in (2,)}
    for dy, pair in ((2, 1), (1, 0), (3, 0), (0, 0), (1, 1), (3, 1), (0, 1)):
        nts[dy, pair] = send_nt(dy, pair)
    normalise(0, 4)
    w_in.wait()
    a2.append(forward_wz(2))
    add_values(0, True)
    a2.append(forward_wz(3))

    a1r[0].wait_recv()
    a3r = send(wb.at[3, rows(0, 256)], wb.at[2, rows(0, 256)], right)
    a1l[0].wait_recv()
    a3l = send(wb.at[1, rows(256, 256)], wb.at[2, rows(256, 256)], left)
    a1r[1].wait_recv()
    a1l[1].wait_recv()
    add_values(1)
    add_values(3)
    add_values(4)
    for pair in a2:
        pair[0].wait_recv()
        pair[1].wait_recv()
    a4r = send(wb.at[7, rows(0, 256)], wb.at[6, rows(0, 256)], right)
    a4l = send(wb.at[5, rows(256, 256)], wb.at[6, rows(256, 256)], left)
    add_values(5)
    add_values(7)
    cot_in.wait()
    cot_z.wait_recv()

    def gradient(dy, pair, write):
        r = rows(256 * pair, 256)

        @pl.loop(0, KV // 256)
        def _(n):
            c = pl.ds(pl.multiple_of(n * 256, 256), 256)
            part = jnp.dot(nt[dy, r, :], cot[:, c], preferred_element_type=F32)
            part += jnp.dot(ntp[dy, r, :], cotp[:, c], preferred_element_type=F32)
            write(c, part)

    d2 = []
    for pair in range(2):
        nts[2, pair].wait_recv()

        def write(c, part, pair=pair):
            sd[rows(256 * pair, 256), c] = part.astype(BF16)

        gradient(2, pair, write)
        there = rows(128 * pair, 128)
        d2.append(send(sd.at[rows(256 * pair, 128)], dr.at[there], right))
        d2.append(send(sd.at[rows(256 * pair + 128, 128)], dl.at[there], left))
    a3r.wait_recv()
    a3l.wait_recv()
    add_values(2)

    def partials(pair):
        top, low = rows(256 * pair, 128), rows(256 * pair + 128, 128)

        def write_right(c, part):
            held[0, :, c] = part[:128]
            sr[low, c] = part[128:].astype(BF16)

        def write_left(c, part):
            sl[top, c] = part[:128].astype(BF16)
            held[1, :, c] = part[128:]

        nts[1, pair].wait_recv()
        gradient(1, pair, write_right)
        nts[3, pair].wait_recv()
        gradient(3, pair, write_left)

    def pass_on(pair):
        there = rows(128 * pair, 128)
        start = 256 * pair
        inside = [p for p in PIECES if start <= p[0] < start + 256]
        upper = [p for p in inside if p[0] < start + 128]
        lower = [p for p in inside if p[0] >= start + 128]
        lefts = [send(sl.at[rows(*p)], rl.at[rows(*p)], left) for p in upper]
        d2[2 * pair].wait_recv()
        top, low = rows(start, 128), rows(start + 128, 128)
        sr[top, :] = (held[0] + dr[there, :].astype(F32)).astype(BF16)
        rights = [send(sr.at[rows(*p)], rr.at[rows(*p)], right) for p in upper + lower]
        d2[2 * pair + 1].wait_recv()
        sl[low, :] = (held[1] + dl[there, :].astype(F32)).astype(BF16)
        lefts += [send(sl.at[rows(*p)], rl.at[rows(*p)], left) for p in lower]
        return list(zip(rights, lefts, strict=True))

    partials(0)
    for copy in (a4r, a4l):
        copy.wait_recv()
    add_values(6)
    arriving = pass_on(0)

    @pl.loop(0, T // 64)
    def _(i):
        r = pl.ds(pl.multiple_of(i * 64, 64), 64)
        total = acc[r, :]
        vout[r, :] = total.astype(BF16)
        inner = jnp.sum(total * cot[r, :].astype(F32), axis=1, keepdims=True) * (1.0 / D)
        slope[r, :] = inner * rstd[r, :]

    def backward(first, last):
        @pl.loop(first, last)
        def _(b):
            for n in range(B // 256):
                c = pl.ds(n * 256, 256)
                g = unpacked(gb[b])[:, n * 256 : (n + 1) * 256]
                dn = lax.dot_general(
                    cot[...], wb[b, c, :], (((1,), (1,)), ((), ())), preferred_element_type=F32
                )
                xf = xb[b, :, c].astype(F32)
                rs = rstd[:, 0:1]
                xb[b, :, c] = (rs * (dn * g - xf * slope[:, 0:1])).astype(BF16)
                share = jnp.sum(dn * xf * rs, axis=0, keepdims=True)
                for i in range(2):
                    ggs[b, 2 * n + i : 2 * n + i + 1, :] = share[:, 128 * i : 128 * (i + 1)]

    ggs[...] = jnp.zeros_like(ggs)
    backward(0, 8)
    gg = [send(ggs.at[i], ggr.at[back(i)], peer(i // 4, i % 4)) for i in range(1, 8)]

    exponents = [exp_ref[i] for i in range(ROUNDS)]
    m_in.wait()
    v_in.wait()
    out1, out2 = [], []

    def own_gradient(pair):
        nts[0, pair].wait_recv()

        def write(c, part):
            own[rows(256 * pair, 256), c] = part

        gradient(0, pair, write)

    def step(p):
        r = rows(*PIECES[p])
        for copy in arriving[p]:
            copy.wait_recv()
        for e in range(8):
            c = pl.ds(128 * e, 128)
            grad = own[r, c] + rr[r, c].astype(F32) + rl[r, c].astype(F32)
            stepped, m_v[r, c], v_v[r, c] = adam(wb[0, r, c].astype(F32), grad, m_v[r, c], v_v[r, c])
            gs[e, r, :] = stepped
        out1.append([send(gs.at[mate_rank(j), r], gr.at[j, r], mate(j)) for j in range(1, 8)])

    mine = pl.ds(pl.multiple_of(rank * 128, 128), 128)

    def mix(p):
        r = rows(*PIECES[p])
        for copy in out1[p]:
            copy.wait_recv()

        start, size = PIECES[p]

        @pl.loop(0, size // 32)
        def _(i):
            q = pl.ds(pl.multiple_of(start + i * 32, 32), 32)
            parts = [gs[rank, q, :].astype(F32)] + [gr[j, q, :].astype(F32) for j in range(1, 8)]
            parts = averaged(parts, exponents)
            for j in range(8):
                gt[j, q, :] = parts[j].astype(BF16)

        out2.append([send(gt.at[j, r], wn.at[r, mine], mate(j)) for j in range(1, 8)])
        wn[r, mine] = gt[0, r, :]

    own_gradient(0)
    partials(1)
    arriving += pass_on(1)
    step(0)
    step(1)
    own_gradient(1)
    mix(0)

    for copy in gg:
        copy.wait_recv()
    total = ggs[0]
    for i in range(1, 8):
        total += ggr[i]
    stepped, first, second = adam(gain_ref[...].astype(F32), unpacked(total), gm_ref[...], gv_ref[...])
    gout[1:2, :] = first
    gout[2:3, :] = second
    gxs[...] = packed(stepped.astype(F32))
    gx = [send(gxs, gxr.at[j], mate(j)) for j in range(1, 8)]

    mix(1)
    step(2)
    for copy in gx:
        copy.wait_recv()
    parts = averaged([gxs[...]] + [gxr[j] for j in range(1, 8)], exponents)
    gout[0:1, :] = unpacked(parts[0])
    mix(2)
    step(3)
    step(4)
    mix(3)
    mix(4)
    for copies in out2:
        for copy in copies:
            copy.wait_recv()

    for copy in sent:
        copy.wait_send()


def write_out(vout, xb, wn, m_v, v_v, gout, val, ig, nw, nm, nv, ng, ngm, ngv, sem):
    f = lax.axis_index("fsdp")
    h, y = f // 4, f % 4
    pairs = [(vout, val.at[0]), (wn, nw.at[0]), (m_v, nm.at[0]), (v_v, nv.at[0])]
    for b in range(8):
        column = ((1 - h if b // 4 else h) * 4 + (y + b % 4) % 4) * B
        pairs.append((xb.at[b], ig.at[0, :, pl.ds(pl.multiple_of(column, B), B)]))
    copies = [pltpu.make_async_copy(src, dst, sem.at[i]) for i, (src, dst) in enumerate(pairs)]
    for copy in copies:
        copy.start()
    ng[...] = gout[0:1, :].astype(BF16)
    ngm[...] = gout[1:2, :]
    ngv[...] = gout[2:3, :]
    for copy in copies:
        copy.wait()


def local(*args):
    any_space, vmem = pl.BlockSpec(memory_space=pl.ANY), pl.BlockSpec(memory_space=pltpu.VMEM)
    smem = pl.BlockSpec(memory_space=pltpu.SMEM)
    shapes = [
        ((1, T, KV), BF16), ((1, T, D), BF16), ((1, B, KV), BF16), ((1, B, KV), F32), ((1, B, KV), F32),
        ((1, B), BF16), ((1, B), F32), ((1, B), F32),
    ]
    held = [
        ((T, KV), BF16), ((8, T, B), BF16), ((B, KV), BF16), ((B, KV), F32), ((B, KV), F32), ((8, B), F32),
    ]
    scratch = [
        ((8, T, B), BF16), ((8, B, T), BF16), ((4, B, T), BF16),
        ((8, B, KV), BF16), ((T, KV), BF16), ((T, KV), BF16),
        ((T, KV), F32), ((B, KV), F32), ((2, 128, KV), F32), ((T, 128), F32), ((T, 128), F32),
        ((8, 8, 128), F32), ((8, 8, 128), F32), ((8, 8, 128), F32), ((8, 128), F32), ((8, 8, 128), F32),
        ((B, KV), BF16), ((B, KV), BF16), ((B, KV), BF16), ((B // 2, KV), BF16), ((B // 2, KV), BF16),
        ((B, KV), BF16), ((B, KV), BF16),
        ((8, B, 128), BF16), ((8, B, 128), BF16), ((8, B, 128), BF16),
    ]
    results = pl.pallas_call(
        kernel,
        out_shape=[pltpu.VMEM(s, t) for s, t in held],
        in_specs=[any_space, vmem, any_space, any_space, any_space, vmem, vmem, any_space, smem],
        out_specs=[vmem] * len(held),
        scratch_shapes=[pltpu.VMEM(s, t) for s, t in scratch]
        + [pltpu.SemaphoreType.DMA((NS,)), pltpu.SemaphoreType.DMA((NS,)), pltpu.SemaphoreType.DMA((NL,))],
        compiler_params=pltpu.CompilerParams(
            collective_id=0, has_side_effects=True, vmem_limit_bytes=46 << 20
        ),
        cost_estimate=pl.CostEstimate(flops=6 * T * D * KV, bytes_accessed=20 << 20, transcendentals=0),
        name="layer_step",
    )(*args)
    return pl.pallas_call(
        write_out,
        out_shape=[jax.ShapeDtypeStruct(s, t) for s, t in shapes],
        in_specs=[vmem] * len(held),
        out_specs=[any_space] * 5 + [vmem] * 3,
        scratch_shapes=[pltpu.SemaphoreType.DMA((12,))],
        compiler_params=pltpu.CompilerParams(vmem_limit_bytes=4 << 20),
        name="write_out",
    )(*[pltpu.with_memory_space_constraint(r, pltpu.VMEM) for r in results])


def solution(mesh):
    split, vector = P("rep", "fsdp", None), P("rep", "fsdp")
    return jax.shard_map(
        local,
        mesh=mesh,
        in_specs=(split, vector, split, split, split, vector, vector, split, P()),
        out_specs=(split, split, split, split, split, vector, vector, vector),
        check_vma=False,
    )
```

```python
import functools

import jax
import jax.numpy as jnp
from jax import lax
from jax.experimental import pallas as pl
from jax.experimental.pallas import tpu as pltpu
from jax.sharding import PartitionSpec as P

STEP = 10
ROUNDS = 4
T = 512
B = 512
D = 4096
KV = 1024
NS = 192
NL = 48
PIECES = ((0, 128), (128, 128), (256, 64), (320, 64), (384, 64), (448, 64))
MESH = pl.DeviceIdType.MESH
F32 = jnp.float32
BF16 = jnp.bfloat16


def adam(param, grad, first, second):
    new_first = 0.9 * first + 0.1 * grad
    new_second = 0.95 * second + 0.05 * grad * grad
    fix_first = 1.0 - 0.9**STEP
    fix_second = 1.0 - 0.95**STEP
    update = new_first / fix_first / (jnp.sqrt(new_second / fix_second) + 1e-08) + 0.1 * param
    return (param - 0.003 * update).astype(BF16), new_first, new_second


def averaged(parts, exponents):
    for e in exponents:
        mixed = []
        for j in range(8):
            partner = jnp.where(e == 0, parts[j ^ 1], jnp.where(e == 1, parts[j ^ 2], parts[j ^ 4]))
            mixed.append(((parts[j] + partner) * 0.5).astype(BF16).astype(F32))
        parts = mixed
    return parts


def packed(row):
    return jnp.concatenate([row[:, 128 * i : 128 * (i + 1)] for i in range(4)] + [jnp.zeros((4, 128), F32)], axis=0)


def unpacked(tile):
    return jnp.concatenate([tile[i : i + 1] for i in range(4)], axis=1)


def kernel(
    x_hbm, gain_ref, w_hbm, m_hbm, v_hbm, gm_ref, gv_ref, cot_hbm, exp_ref,
    vout, xb, wn, m_v, v_v, gout,
    nrm, nt, ntp, wb, cot, cotp, acc, own, held, rstd, slope,
    gb, ggs, ggr, gxs, gxr,
    sd, sr, sl, dr, dl, rr, rl, gs, gr, gt, gf,
    ssem, rsem, lsem,
):
    rep = lax.axis_index("rep")
    f = lax.axis_index("fsdp")
    h, y = f // 4, f % 4
    zlo, rank = rep // 8, rep % 8
    bits = (rank % 2, (rank // 2) % 2, rank // 4)

    def shard(dh, dy):
        return (1 - h if dh else h) * 4 + (y + dy) % 4

    def peer(dh, dy):
        return (rep, shard(dh, dy))

    def mate_rank(j):
        return sum((1 - b if (j >> i) & 1 else b) * (1 << i) for i, b in enumerate(bits))

    def mate(j):
        return (zlo * 8 + mate_rank(j), f)

    right, left, across = peer(0, 1), peer(0, 3), peer(1, 0)

    sent, kept = [], []

    def send(src, dst, device):
        i = len(sent)
        copy = pltpu.make_async_remote_copy(
            src_ref=src, dst_ref=dst, send_sem=ssem.at[i], recv_sem=rsem.at[i],
            device_id=device, device_id_type=MESH,
        )
        copy.start()
        sent.append(copy)
        return copy

    def settle(last):
        while settled[0] < last:
            sent[settled[0]].wait_send()
            settled[0] += 1

    settled = [0]

    def move(src, dst):
        copy = pltpu.make_async_copy(src, dst, lsem.at[len(kept)])
        copy.start()
        kept.append(copy)
        return copy

    def rows(start, size):
        return pl.ds(start, size)

    barrier = pltpu.get_barrier_semaphore()
    others = [peer(i // 4, i % 4) for i in range(1, 8)] + [mate(j) for j in range(1, 8)]
    for device in others:
        pl.semaphore_signal(barrier, inc=1, device_id=device, device_id_type=MESH)
    pl.semaphore_wait(barrier, len(others))

    def back(i):
        return 4 * (i // 4) + (4 - i % 4) % 4

    gb[0] = packed(gain_ref[...].astype(F32))
    gains = [send(gb.at[0], gb.at[back(i)], peer(i // 4, i % 4)) for i in range(1, 8)]

    a1r, a1l, wz = [], [], []
    for k in range(2):
        for pieces, slot, half, device in ((a1r, 3, k, right), (a1l, 1, 1 - k, left)):
            r = rows(256 * half, 256)
            pieces.append(send(w_hbm.at[0, r], wb.at[slot, r], device))
        for q in (2 * k, 2 * k + 1):
            r = rows(128 * q, 128)
            wz.append(send(w_hbm.at[0, r], wb.at[4, r], across))
    cot_z = send(cot_hbm.at[0], cotp, across)

    def columns(b):
        return pl.ds(pl.multiple_of(shard(b // 4, b % 4) * B, B), B)

    x_in = [move(x_hbm.at[0, :, columns(b)], xb.at[b]) for b in range(8)]
    cot_in = move(cot_hbm.at[0], cot)
    w_in = move(w_hbm.at[0], wb.at[0])
    m_in = move(m_hbm.at[0], m_v)
    v_in = move(v_hbm.at[0], v_v)
    for copy in x_in:
        copy.wait()

    @pl.loop(0, T // 64)
    def _(i):
        r = pl.ds(pl.multiple_of(i * 64, 64), 64)
        total = jnp.zeros((64, B), F32)
        for b in range(8):
            xf = xb[b, r, :].astype(F32)
            total += xf * xf
        mean = jnp.sum(total, axis=1, keepdims=True) * (1.0 / D)
        rstd[r, :] = jnp.broadcast_to(lax.rsqrt(mean + 1e-05), (64, 128))

    for copy in gains:
        copy.wait_recv()

    def normalise(first, last):
        @pl.loop(first, last)
        def _(b):
            g = unpacked(gb[b])

            @pl.loop(0, T // 128)
            def _(i):
                r = pl.ds(pl.multiple_of(i * 128, 128), 128)
                tile = (xb[b, r, :].astype(F32) * rstd[r, 0:1] * g).astype(BF16)
                nrm[b, r, :] = tile
                nt[b, :, r] = tile.T

    def forward_wz(k):
        wz[k].wait_recv()
        piece = rows(128 * k, 128)
        return (
            send(wb.at[4, piece], wb.at[7, piece], right),
            send(wb.at[4, piece], wb.at[5, piece], left),
        )

    def add_values(b, first=False):
        @pl.loop(0, KV // 256)
        def _(n):
            c = pl.ds(pl.multiple_of(n * 256, 256), 256)
            part = jnp.dot(nrm[b], wb[b, :, c], preferred_element_type=F32)
            acc[:, c] = part if first else acc[:, c] + part

    def send_nt(dy, pair):
        r = rows(256 * pair, 256)
        return send(nt.at[4 + dy, r], ntp.at[dy, r], across)

    a2 = [forward_wz(0)]
    normalise(4, 8)
    a2.append(forward_wz(1))
    nts = {(dy, 0): send_nt(dy, 0) for dy in (2,)}
    for dy, pair in ((2, 1), (1, 0), (3, 0), (0, 0), (1, 1), (3, 1), (0, 1)):
        nts[dy, pair] = send_nt(dy, pair)
    normalise(0, 4)
    w_in.wait()
    a2.append(forward_wz(2))
    add_values(0, True)
    a2.append(forward_wz(3))

    a1r[0].wait_recv()
    a3r = send(wb.at[3, rows(0, 256)], wb.at[2, rows(0, 256)], right)
    a1l[0].wait_recv()
    a3l = send(wb.at[1, rows(256, 256)], wb.at[2, rows(256, 256)], left)
    a1r[1].wait_recv()
    a1l[1].wait_recv()
    add_values(1)
    add_values(3)
    add_values(4)
    for pair in a2:
        pair[0].wait_recv()
        pair[1].wait_recv()
    a4r = send(wb.at[7, rows(0, 256)], wb.at[6, rows(0, 256)], right)
    a4l = send(wb.at[5, rows(256, 256)], wb.at[6, rows(256, 256)], left)
    add_values(5)
    add_values(7)
    cot_in.wait()
    cot_z.wait_recv()

    def gradient(dy, pair, write):
        r = rows(256 * pair, 256)

        @pl.loop(0, KV // 256)
        def _(n):
            c = pl.ds(pl.multiple_of(n * 256, 256), 256)
            part = jnp.dot(nt[dy, r, :], cot[:, c], preferred_element_type=F32)
            part += jnp.dot(ntp[dy, r, :], cotp[:, c], preferred_element_type=F32)
            write(c, part)

    def far_gradient(pair):
        nts[2, pair].wait_recv()

        def write(c, part):
            sd[rows(256 * pair, 256), c] = part.astype(BF16)

        gradient(2, pair, write)

    d2 = {}

    def send_far(pair):
        d2[pair] = []
        for start in (0, 64):
            there = rows(128 * pair + start, 64)
            top, low = rows(256 * pair + start, 64), rows(256 * pair + 128 + start, 64)
            d2[pair].append((send(sd.at[top], dr.at[there], right), send(sd.at[low], dl.at[there], left)))

    far_gradient(0)
    send_far(0)
    far_gradient(1)
    a3r.wait_recv()
    a3l.wait_recv()
    add_values(2)

    def partial_right(pair):
        def write(c, part):
            held[0, :, c] = part[:128]
            sr[rows(256 * pair + 128, 128), c] = part[128:].astype(BF16)

        nts[1, pair].wait_recv()
        gradient(1, pair, write)

    def partial_left(pair):
        def write(c, part):
            sl[rows(256 * pair, 128), c] = part[:128].astype(BF16)
            held[1, :, c] = part[128:]

        nts[3, pair].wait_recv()
        gradient(3, pair, write)

    arriving = {}

    def to_right(start):
        r = rows(start, 64)
        arriving[start].append(send(sr.at[r], rr.at[r], right))

    def to_left(start):
        r = rows(start, 64)
        arriving[start].append(send(sl.at[r], rl.at[r], left))

    def sum_right(pair, k):
        d2[pair][k][0].wait_recv()
        start = 256 * pair + 64 * k
        far = dr[rows(128 * pair + 64 * k, 64), :].astype(F32)
        sr[rows(start, 64), :] = (held[0, rows(64 * k, 64), :] + far).astype(BF16)
        to_right(start)

    def sum_left(pair, k):
        d2[pair][k][1].wait_recv()
        start = 256 * pair + 128 + 64 * k
        far = dl[rows(128 * pair + 64 * k, 64), :].astype(F32)
        sl[rows(start, 64), :] = (held[1, rows(64 * k, 64), :] + far).astype(BF16)
        to_left(start)

    def pass_on(pair, between):
        start = 256 * pair
        for k in range(4):
            arriving[start + 64 * k] = []
        to_left(start)
        to_left(start + 64)
        sum_right(pair, 0)
        sum_left(pair, 0)
        between()
        sum_right(pair, 1)
        to_right(start + 128)
        to_right(start + 192)
        sum_left(pair, 1)

    partial_right(0)
    partial_left(0)
    for copy in (a4r, a4l):
        copy.wait_recv()

    def middle():
        add_values(6)

    pass_on(0, middle)
    send_far(1)

    @pl.loop(0, T // 64)
    def _(i):
        r = pl.ds(pl.multiple_of(i * 64, 64), 64)
        total = acc[r, :]
        vout[r, :] = total.astype(BF16)
        inner = jnp.sum(total * cot[r, :].astype(F32), axis=1, keepdims=True) * (1.0 / D)
        slope[r, :] = inner * rstd[r, :]

    def backward(first, last):
        @pl.loop(first, last)
        def _(b):
            for n in range(B // 256):
                c = pl.ds(n * 256, 256)
                g = unpacked(gb[b])[:, n * 256 : (n + 1) * 256]
                dn = lax.dot_general(
                    cot[...], wb[b, c, :], (((1,), (1,)), ((), ())), preferred_element_type=F32
                )
                xf = xb[b, :, c].astype(F32)
                rs = rstd[:, 0:1]
                xb[b, :, c] = (rs * (dn * g - xf * slope[:, 0:1])).astype(BF16)
                share = jnp.sum(dn * xf * rs, axis=0, keepdims=True)
                for i in range(2):
                    ggs[b, 2 * n + i : 2 * n + i + 1, :] = share[:, 128 * i : 128 * (i + 1)]

    ggs[...] = jnp.zeros_like(ggs)
    backward(0, 4)

    exponents = [exp_ref[i] for i in range(ROUNDS)]
    m_in.wait()
    v_in.wait()
    out1, out2 = [], []

    def own_gradient(pair):
        nts[0, pair].wait_recv()

        def write(c, part):
            own[rows(256 * pair, 256), c] = part

        gradient(0, pair, write)

    def step(p):
        r = rows(*PIECES[p])
        for start in range(PIECES[p][0], sum(PIECES[p]), 64):
            for copy in arriving[start]:
                copy.wait_recv()
        for e in range(8):
            c = pl.ds(128 * e, 128)
            grad = own[r, c] + rr[r, c].astype(F32) + rl[r, c].astype(F32)
            stepped, m_v[r, c], v_v[r, c] = adam(wb[0, r, c].astype(F32), grad, m_v[r, c], v_v[r, c])
            gs[e, r, :] = stepped
        out1.append([send(gs.at[mate_rank(j), r], gr.at[j, r], mate(j)) for j in range(1, 8)])

    def mix(p):
        r = rows(*PIECES[p])
        for copy in out1[p]:
            copy.wait_recv()

        start, size = PIECES[p]

        @pl.loop(0, size // 32)
        def _(i):
            q = pl.ds(pl.multiple_of(start + i * 32, 32), 32)
            parts = [gs[rank, q, :].astype(F32)] + [gr[j, q, :].astype(F32) for j in range(1, 8)]
            parts = averaged(parts, exponents)
            for j in range(8):
                gt[j, q, :] = parts[j].astype(BF16)

        out2.append([send(gt.at[j, r], gf.at[rank, r], mate(j)) for j in range(1, 8)])
        gf[rank, r, :] = gt[0, r, :]

    def finish(p):
        r = rows(*PIECES[p])
        for copy in out2[p]:
            copy.wait_recv()
        for e in range(8):
            wn[r, 128 * e : 128 * (e + 1)] = gf[e, r, :]

    own_gradient(0)
    step(0)
    backward(4, 8)
    gg = [send(ggs.at[i], ggr.at[back(i)], peer(i // 4, i % 4)) for i in range(1, 8)]
    partial_right(1)
    step(1)
    partial_left(1)
    early = len(sent)
    pass_on(1, lambda: mix(0))
    ready = len(sent)
    own_gradient(1)
    mix(1)
    settle(early)

    for copy in gg:
        copy.wait_recv()
    total = ggs[0]
    for i in range(1, 8):
        total += ggr[i]
    stepped, first, second = adam(gain_ref[...].astype(F32), unpacked(total), gm_ref[...], gv_ref[...])
    gout[1:2, :] = first
    gout[2:3, :] = second
    gxs[...] = packed(stepped.astype(F32))
    gx = [send(gxs, gxr.at[j], mate(j)) for j in range(1, 8)]

    step(2)
    finish(0)
    step(3)
    for copy in gx:
        copy.wait_recv()
    parts = averaged([gxs[...]] + [gxr[j] for j in range(1, 8)], exponents)
    gout[0:1, :] = unpacked(parts[0])
    finish(1)
    step(4)
    step(5)
    mix(2)
    mix(3)
    settle(ready)
    mix(4)
    mix(5)
    settle(len(sent) - 28)
    for p in range(2, len(PIECES)):
        finish(p)

    settle(len(sent))


def write_out(vout, xb, wn, m_v, v_v, gout, val, ig, nw, nm, nv, ng, ngm, ngv, sem):
    f = lax.axis_index("fsdp")
    h, y = f // 4, f % 4
    pairs = [(vout, val.at[0]), (wn, nw.at[0]), (m_v, nm.at[0]), (v_v, nv.at[0])]
    for b in range(8):
        column = ((1 - h if b // 4 else h) * 4 + (y + b % 4) % 4) * B
        pairs.append((xb.at[b], ig.at[0, :, pl.ds(pl.multiple_of(column, B), B)]))
    copies = [pltpu.make_async_copy(src, dst, sem.at[i]) for i, (src, dst) in enumerate(pairs)]
    for copy in copies:
        copy.start()
    ng[...] = gout[0:1, :].astype(BF16)
    ngm[...] = gout[1:2, :]
    ngv[...] = gout[2:3, :]
    for copy in copies:
        copy.wait()


def local(*args):
    any_space, vmem = pl.BlockSpec(memory_space=pl.ANY), pl.BlockSpec(memory_space=pltpu.VMEM)
    smem = pl.BlockSpec(memory_space=pltpu.SMEM)
    shapes = [
        ((1, T, KV), BF16), ((1, T, D), BF16), ((1, B, KV), BF16), ((1, B, KV), F32), ((1, B, KV), F32),
        ((1, B), BF16), ((1, B), F32), ((1, B), F32),
    ]
    held = [
        ((T, KV), BF16), ((8, T, B), BF16), ((B, KV), BF16), ((B, KV), F32), ((B, KV), F32), ((8, B), F32),
    ]
    scratch = [
        ((8, T, B), BF16), ((8, B, T), BF16), ((4, B, T), BF16),
        ((8, B, KV), BF16), ((T, KV), BF16), ((T, KV), BF16),
        ((T, KV), F32), ((B, KV), F32), ((2, 128, KV), F32), ((T, 128), F32), ((T, 128), F32),
        ((8, 8, 128), F32), ((8, 8, 128), F32), ((8, 8, 128), F32), ((8, 128), F32), ((8, 8, 128), F32),
        ((B, KV), BF16), ((B, KV), BF16), ((B, KV), BF16), ((B // 2, KV), BF16), ((B // 2, KV), BF16),
        ((B, KV), BF16), ((B, KV), BF16),
        ((8, B, 128), BF16), ((8, B, 128), BF16), ((8, B, 128), BF16), ((8, B, 128), BF16),
    ]
    results = pl.pallas_call(
        kernel,
        out_shape=[pltpu.VMEM(s, t) for s, t in held],
        in_specs=[any_space, vmem, any_space, any_space, any_space, vmem, vmem, any_space, smem],
        out_specs=[vmem] * len(held),
        scratch_shapes=[pltpu.VMEM(s, t) for s, t in scratch]
        + [pltpu.SemaphoreType.DMA((NS,)), pltpu.SemaphoreType.DMA((NS,)), pltpu.SemaphoreType.DMA((NL,))],
        compiler_params=pltpu.CompilerParams(
            collective_id=0, has_side_effects=True, vmem_limit_bytes=46 << 20
        ),
        cost_estimate=pl.CostEstimate(flops=6 * T * D * KV, bytes_accessed=20 << 20, transcendentals=0),
        name="layer_step",
    )(*args)
    return pl.pallas_call(
        write_out,
        out_shape=[jax.ShapeDtypeStruct(s, t) for s, t in shapes],
        in_specs=[vmem] * len(held),
        out_specs=[any_space] * 5 + [vmem] * 3,
        scratch_shapes=[pltpu.SemaphoreType.DMA((12,))],
        compiler_params=pltpu.CompilerParams(vmem_limit_bytes=4 << 20),
        name="write_out",
    )(*[pltpu.with_memory_space_constraint(r, pltpu.VMEM) for r in results])


def solution(mesh):
    split, vector = P("rep", "fsdp", None), P("rep", "fsdp")
    return jax.shard_map(
        local,
        mesh=mesh,
        in_specs=(split, vector, split, split, split, vector, vector, split, P()),
        out_specs=(split, split, split, split, split, vector, vector, vector),
        check_vma=False,
    )
```

```python
import functools

import jax
import jax.numpy as jnp
from jax import lax
from jax.experimental import pallas as pl
from jax.experimental.pallas import tpu as pltpu
from jax.sharding import PartitionSpec as P

STEP = 10
ROUNDS = 4
T = 512
B = 512
D = 4096
KV = 1024
NS = 192
NL = 48
PIECES = ((0, 128), (128, 128), (256, 64), (320, 64), (384, 64), (448, 64))
MESH = pl.DeviceIdType.MESH
F32 = jnp.float32
BF16 = jnp.bfloat16


def adam(param, grad, first, second):
    new_first = 0.9 * first + 0.1 * grad
    new_second = 0.95 * second + 0.05 * grad * grad
    fix_first = 1.0 - 0.9**STEP
    fix_second = 1.0 - 0.95**STEP
    update = new_first / fix_first / (jnp.sqrt(new_second / fix_second) + 1e-08) + 0.1 * param
    return (param - 0.003 * update).astype(BF16), new_first, new_second


def averaged(parts, exponents):
    for e in exponents:
        mixed = []
        for j in range(8):
            partner = jnp.where(e == 0, parts[j ^ 1], jnp.where(e == 1, parts[j ^ 2], parts[j ^ 4]))
            mixed.append(((parts[j] + partner) * 0.5).astype(BF16).astype(F32))
        parts = mixed
    return parts


def packed(row):
    return jnp.concatenate([row[:, 128 * i : 128 * (i + 1)] for i in range(4)] + [jnp.zeros((4, 128), F32)], axis=0)


def unpacked(tile):
    return jnp.concatenate([tile[i : i + 1] for i in range(4)], axis=1)


def kernel(
    x_hbm, gain_ref, w_hbm, m_hbm, v_hbm, gm_ref, gv_ref, cot_hbm, exp_ref,
    vout, xb, wn, m_v, v_v, gout,
    nrm, nt, ntp, wb, cot, cotp, acc, own, held, rstd, slope,
    gb, ggs, ggr, gxs, gxr,
    sd, sr, sl, dr, dl, rr, rl, gs, gr, gt, gf,
    ssem, rsem, lsem,
):
    rep = lax.axis_index("rep")
    f = lax.axis_index("fsdp")
    h, y = f // 4, f % 4
    zlo, rank = rep // 8, rep % 8
    bits = (rank % 2, (rank // 2) % 2, rank // 4)

    def shard(dh, dy):
        return (1 - h if dh else h) * 4 + (y + dy) % 4

    def peer(dh, dy):
        return (rep, shard(dh, dy))

    def mate_rank(j):
        return sum((1 - b if (j >> i) & 1 else b) * (1 << i) for i, b in enumerate(bits))

    def mate(j):
        return (zlo * 8 + mate_rank(j), f)

    right, left, across = peer(0, 1), peer(0, 3), peer(1, 0)

    sent, kept = [], []

    def send(src, dst, device):
        i = len(sent)
        copy = pltpu.make_async_remote_copy(
            src_ref=src, dst_ref=dst, send_sem=ssem.at[i], recv_sem=rsem.at[i],
            device_id=device, device_id_type=MESH,
        )
        copy.start()
        sent.append(copy)
        return copy

    def settle(last):
        while settled[0] < last:
            sent[settled[0]].wait_send()
            settled[0] += 1

    settled = [0]

    def move(src, dst):
        copy = pltpu.make_async_copy(src, dst, lsem.at[len(kept)])
        copy.start()
        kept.append(copy)
        return copy

    def rows(start, size):
        return pl.ds(start, size)

    barrier = pltpu.get_barrier_semaphore()
    others = [peer(i // 4, i % 4) for i in range(1, 8)] + [mate(j) for j in range(1, 8)]
    for device in others:
        pl.semaphore_signal(barrier, inc=1, device_id=device, device_id_type=MESH)
    pl.semaphore_wait(barrier, len(others))

    def back(i):
        return 4 * (i // 4) + (4 - i % 4) % 4

    a1r, a1l, wz = [], [], []
    for k in range(2):
        for pieces, slot, half, device in ((a1r, 3, k, right), (a1l, 1, 1 - k, left)):
            r = rows(256 * half, 256)
            pieces.append(send(w_hbm.at[0, r], wb.at[slot, r], device))
        for q in (2 * k, 2 * k + 1):
            r = rows(128 * q, 128)
            wz.append(send(w_hbm.at[0, r], wb.at[4, r], across))
        if k == 0:
            gb[0] = packed(gain_ref[...].astype(F32))
            gains = [send(gb.at[0], gb.at[back(i)], peer(i // 4, i % 4)) for i in range(1, 8)]
    cot_z = send(cot_hbm.at[0], cotp, across)

    def columns(b):
        return pl.ds(pl.multiple_of(shard(b // 4, b % 4) * B, B), B)

    x_in = [move(x_hbm.at[0, :, columns(b)], xb.at[b]) for b in range(8)]
    cot_in = move(cot_hbm.at[0], cot)
    w_in = move(w_hbm.at[0], wb.at[0])
    m_in = move(m_hbm.at[0], m_v)
    v_in = move(v_hbm.at[0], v_v)
    for copy in x_in:
        copy.wait()

    @pl.loop(0, T // 64)
    def _(i):
        r = pl.ds(pl.multiple_of(i * 64, 64), 64)
        total = jnp.zeros((64, B), F32)
        for b in range(8):
            xf = xb[b, r, :].astype(F32)
            total += xf * xf
        mean = jnp.sum(total, axis=1, keepdims=True) * (1.0 / D)
        rstd[r, :] = jnp.broadcast_to(lax.rsqrt(mean + 1e-05), (64, 128))

    for copy in gains:
        copy.wait_recv()

    def normalise(first, last):
        @pl.loop(first, last)
        def _(b):
            g = unpacked(gb[b])

            @pl.loop(0, T // 128)
            def _(i):
                r = pl.ds(pl.multiple_of(i * 128, 128), 128)
                tile = (xb[b, r, :].astype(F32) * rstd[r, 0:1] * g).astype(BF16)
                nrm[b, r, :] = tile
                nt[b, :, r] = tile.T

    def forward_wz(k):
        wz[k].wait_recv()
        piece = rows(128 * k, 128)
        return (
            send(wb.at[4, piece], wb.at[7, piece], right),
            send(wb.at[4, piece], wb.at[5, piece], left),
        )

    def add_values(b, first=False):
        @pl.loop(0, KV // 256)
        def _(n):
            c = pl.ds(pl.multiple_of(n * 256, 256), 256)
            part = jnp.dot(nrm[b], wb[b, :, c], preferred_element_type=F32)
            acc[:, c] = part if first else acc[:, c] + part

    def send_nt(dy, pair):
        r = rows(256 * pair, 256)
        return send(nt.at[4 + dy, r], ntp.at[dy, r], across)

    a2 = [forward_wz(0)]
    normalise(4, 8)
    a2.append(forward_wz(1))
    nts = {(dy, 0): send_nt(dy, 0) for dy in (2,)}
    for dy, pair in ((2, 1), (1, 0), (3, 0), (0, 0), (1, 1), (3, 1), (0, 1)):
        nts[dy, pair] = send_nt(dy, pair)
    normalise(0, 4)
    w_in.wait()
    a2.append(forward_wz(2))
    add_values(0, True)
    a2.append(forward_wz(3))

    a1r[0].wait_recv()
    a3r = send(wb.at[3, rows(0, 256)], wb.at[2, rows(0, 256)], right)
    a1l[0].wait_recv()
    a3l = send(wb.at[1, rows(256, 256)], wb.at[2, rows(256, 256)], left)
    a1r[1].wait_recv()
    a1l[1].wait_recv()
    add_values(1)
    add_values(3)
    add_values(4)
    for pair in a2:
        pair[0].wait_recv()
        pair[1].wait_recv()
    a4r = send(wb.at[7, rows(0, 192)], wb.at[6, rows(0, 192)], right)
    a4l = send(wb.at[5, rows(320, 192)], wb.at[6, rows(320, 192)], left)
    add_values(5)
    add_values(7)
    cot_in.wait()
    cot_z.wait_recv()

    def gradient(dy, pair, write):
        r = rows(256 * pair, 256)

        @pl.loop(0, KV // 256)
        def _(n):
            c = pl.ds(pl.multiple_of(n * 256, 256), 256)
            part = jnp.dot(nt[dy, r, :], cot[:, c], preferred_element_type=F32)
            part += jnp.dot(ntp[dy, r, :], cotp[:, c], preferred_element_type=F32)
            write(c, part)

    def far_gradient(pair):
        nts[2, pair].wait_recv()

        def write(c, part):
            sd[rows(256 * pair, 256), c] = part.astype(BF16)

        gradient(2, pair, write)

    d2 = {}

    def send_far(pair):
        d2[pair] = []
        for start in (0, 64):
            there = rows(128 * pair + start, 64)
            top, low = rows(256 * pair + start, 64), rows(256 * pair + 128 + start, 64)
            d2[pair].append((send(sd.at[top], dr.at[there], right), send(sd.at[low], dl.at[there], left)))

    far_gradient(0)
    send_far(0)
    far_gradient(1)
    a3r.wait_recv()
    a3l.wait_recv()
    a4z = send(wb.at[2, rows(192, 128)], wb.at[6, rows(192, 128)], across)
    add_values(2)

    def partial_right(pair):
        def write(c, part):
            held[0, :, c] = part[:128]
            sr[rows(256 * pair + 128, 128), c] = part[128:].astype(BF16)

        nts[1, pair].wait_recv()
        gradient(1, pair, write)

    def partial_left(pair):
        def write(c, part):
            sl[rows(256 * pair, 128), c] = part[:128].astype(BF16)
            held[1, :, c] = part[128:]

        nts[3, pair].wait_recv()
        gradient(3, pair, write)

    arriving = {}

    def to_right(start):
        r = rows(start, 64)
        arriving[start].append(send(sr.at[r], rr.at[r], right))

    def to_left(start):
        r = rows(start, 64)
        arriving[start].append(send(sl.at[r], rl.at[r], left))

    def sum_right(pair, k):
        d2[pair][k][0].wait_recv()
        start = 256 * pair + 64 * k
        far = dr[rows(128 * pair + 64 * k, 64), :].astype(F32)
        sr[rows(start, 64), :] = (held[0, rows(64 * k, 64), :] + far).astype(BF16)
        to_right(start)

    def sum_left(pair, k):
        d2[pair][k][1].wait_recv()
        start = 256 * pair + 128 + 64 * k
        far = dl[rows(128 * pair + 64 * k, 64), :].astype(F32)
        sl[rows(start, 64), :] = (held[1, rows(64 * k, 64), :] + far).astype(BF16)
        to_left(start)

    def pass_on(pair, between):
        start = 256 * pair
        for k in range(4):
            arriving[start + 64 * k] = []
        to_left(start)
        to_left(start + 64)
        sum_right(pair, 0)
        sum_left(pair, 0)
        between()
        sum_right(pair, 1)
        to_right(start + 128)
        to_right(start + 192)
        sum_left(pair, 1)

    partial_right(0)
    partial_left(0)
    pass_on(0, lambda: None)
    send_far(1)

    def slopes():
        @pl.loop(0, T // 64)
        def _(i):
            r = pl.ds(pl.multiple_of(i * 64, 64), 64)
            total = acc[r, :]
            vout[r, :] = total.astype(BF16)
            inner = jnp.sum(total * cot[r, :].astype(F32), axis=1, keepdims=True) * (1.0 / D)
            slope[r, :] = inner * rstd[r, :]

    def product(b, n):
        c = pl.ds(n * 256, 256)
        return lax.dot_general(
            cot[...], wb[b, c, :], (((1,), (1,)), ((), ())), preferred_element_type=F32
        )

    def gain_shares(first, last):
        @pl.loop(first, last)
        def _(b):
            for n in range(B // 256):
                xf = xb[b, :, n * 256 : (n + 1) * 256].astype(F32)
                share = jnp.sum(product(b, n) * xf * rstd[:, 0:1], axis=0, keepdims=True)
                for i in range(2):
                    ggs[b, 2 * n + i : 2 * n + i + 1, :] = share[:, 128 * i : 128 * (i + 1)]

    def backward(first, last):
        @pl.loop(first, last)
        def _(b):
            for n in range(B // 256):
                c = pl.ds(n * 256, 256)
                g = unpacked(gb[b])[:, n * 256 : (n + 1) * 256]
                xf = xb[b, :, c].astype(F32)
                xb[b, :, c] = (rstd[:, 0:1] * (product(b, n) * g - xf * slope[:, 0:1])).astype(BF16)

    ggs[...] = jnp.zeros_like(ggs)
    gain_shares(0, 6)
    gain_shares(7, 8)
    gg = [send(ggs.at[i], ggr.at[back(i)], peer(i // 4, i % 4)) for i in (1, 2, 3, 4, 5, 7)]

    exponents = [exp_ref[i] for i in range(ROUNDS)]
    m_in.wait()
    v_in.wait()
    out1, out2 = [], []

    def own_gradient(pair):
        nts[0, pair].wait_recv()

        def write(c, part):
            own[rows(256 * pair, 256), c] = part

        gradient(0, pair, write)

    def step(p):
        r = rows(*PIECES[p])
        for start in range(PIECES[p][0], sum(PIECES[p]), 64):
            for copy in arriving[start]:
                copy.wait_recv()
        for e in range(8):
            c = pl.ds(128 * e, 128)
            grad = own[r, c] + rr[r, c].astype(F32) + rl[r, c].astype(F32)
            stepped, m_v[r, c], v_v[r, c] = adam(wb[0, r, c].astype(F32), grad, m_v[r, c], v_v[r, c])
            gs[e, r, :] = stepped
        out1.append([send(gs.at[mate_rank(j), r], gr.at[j, r], mate(j)) for j in range(1, 8)])

    def mix(p):
        r = rows(*PIECES[p])
        for copy in out1[p]:
            copy.wait_recv()

        start, size = PIECES[p]

        @pl.loop(0, size // 32)
        def _(i):
            q = pl.ds(pl.multiple_of(start + i * 32, 32), 32)
            parts = [gs[rank, q, :].astype(F32)] + [gr[j, q, :].astype(F32) for j in range(1, 8)]
            parts = averaged(parts, exponents)
            for j in range(8):
                gt[j, q, :] = parts[j].astype(BF16)

        out2.append([send(gt.at[j, r], gf.at[rank, r], mate(j)) for j in range(1, 8)])
        gf[rank, r, :] = gt[0, r, :]

    def finish(p):
        r = rows(*PIECES[p])
        for copy in out2[p]:
            copy.wait_recv()
        for e in range(8):
            wn[r, 128 * e : 128 * (e + 1)] = gf[e, r, :]

    own_gradient(0)
    step(0)
    partial_right(1)
    step(1)
    partial_left(1)
    early = len(sent)
    pass_on(1, lambda: mix(0))
    ready = len(sent)
    own_gradient(1)
    mix(1)
    settle(early)
    step(2)
    step(3)
    for copy in (a4r, a4l, a4z):
        copy.wait_recv()
    add_values(6)
    gain_shares(6, 7)
    gg.append(send(ggs.at[6], ggr.at[back(6)], peer(1, 2)))
    step(4)
    slopes()
    step(5)

    mix(2)
    mix(3)

    for copy in gg:
        copy.wait_recv()
    total = ggs[0]
    for i in range(1, 8):
        total += ggr[i]
    stepped, first, second = adam(gain_ref[...].astype(F32), unpacked(total), gm_ref[...], gv_ref[...])
    gout[1:2, :] = first
    gout[2:3, :] = second
    gxs[...] = packed(stepped.astype(F32))
    gx = [send(gxs, gxr.at[j], mate(j)) for j in range(1, 8)]

    backward(0, 2)
    mix(4)
    mix(5)
    for p in range(2):
        finish(p)
    backward(2, 8)
    for copy in gx:
        copy.wait_recv()
    parts = averaged([gxs[...]] + [gxr[j] for j in range(1, 8)], exponents)
    gout[0:1, :] = unpacked(parts[0])
    settle(len(sent) - 28)
    for p in range(2, len(PIECES)):
        finish(p)

    settle(len(sent))


def write_out(vout, xb, wn, m_v, v_v, gout, val, ig, nw, nm, nv, ng, ngm, ngv, sem):
    f = lax.axis_index("fsdp")
    h, y = f // 4, f % 4
    pairs = [(vout, val.at[0]), (wn, nw.at[0]), (m_v, nm.at[0]), (v_v, nv.at[0])]
    for b in range(8):
        column = ((1 - h if b // 4 else h) * 4 + (y + b % 4) % 4) * B
        pairs.append((xb.at[b], ig.at[0, :, pl.ds(pl.multiple_of(column, B), B)]))
    copies = [pltpu.make_async_copy(src, dst, sem.at[i]) for i, (src, dst) in enumerate(pairs)]
    for copy in copies:
        copy.start()
    ng[...] = gout[0:1, :].astype(BF16)
    ngm[...] = gout[1:2, :]
    ngv[...] = gout[2:3, :]
    for copy in copies:
        copy.wait()


def local(*args):
    any_space, vmem = pl.BlockSpec(memory_space=pl.ANY), pl.BlockSpec(memory_space=pltpu.VMEM)
    smem = pl.BlockSpec(memory_space=pltpu.SMEM)
    shapes = [
        ((1, T, KV), BF16), ((1, T, D), BF16), ((1, B, KV), BF16), ((1, B, KV), F32), ((1, B, KV), F32),
        ((1, B), BF16), ((1, B), F32), ((1, B), F32),
    ]
    held = [
        ((T, KV), BF16), ((8, T, B), BF16), ((B, KV), BF16), ((B, KV), F32), ((B, KV), F32), ((8, B), F32),
    ]
    scratch = [
        ((8, T, B), BF16), ((8, B, T), BF16), ((4, B, T), BF16),
        ((8, B, KV), BF16), ((T, KV), BF16), ((T, KV), BF16),
        ((T, KV), F32), ((B, KV), F32), ((2, 128, KV), F32), ((T, 128), F32), ((T, 128), F32),
        ((8, 8, 128), F32), ((8, 8, 128), F32), ((8, 8, 128), F32), ((8, 128), F32), ((8, 8, 128), F32),
        ((B, KV), BF16), ((B, KV), BF16), ((B, KV), BF16), ((B // 2, KV), BF16), ((B // 2, KV), BF16),
        ((B, KV), BF16), ((B, KV), BF16),
        ((8, B, 128), BF16), ((8, B, 128), BF16), ((8, B, 128), BF16), ((8, B, 128), BF16),
    ]
    results = pl.pallas_call(
        kernel,
        out_shape=[pltpu.VMEM(s, t) for s, t in held],
        in_specs=[any_space, vmem, any_space, any_space, any_space, vmem, vmem, any_space, smem],
        out_specs=[vmem] * len(held),
        scratch_shapes=[pltpu.VMEM(s, t) for s, t in scratch]
        + [pltpu.SemaphoreType.DMA((NS,)), pltpu.SemaphoreType.DMA((NS,)), pltpu.SemaphoreType.DMA((NL,))],
        compiler_params=pltpu.CompilerParams(
            collective_id=0, has_side_effects=True, vmem_limit_bytes=46 << 20
        ),
        cost_estimate=pl.CostEstimate(flops=6 * T * D * KV, bytes_accessed=20 << 20, transcendentals=0),
        name="layer_step",
    )(*args)
    return pl.pallas_call(
        write_out,
        out_shape=[jax.ShapeDtypeStruct(s, t) for s, t in shapes],
        in_specs=[vmem] * len(held),
        out_specs=[any_space] * 5 + [vmem] * 3,
        scratch_shapes=[pltpu.SemaphoreType.DMA((12,))],
        compiler_params=pltpu.CompilerParams(vmem_limit_bytes=4 << 20),
        name="write_out",
    )(*[pltpu.with_memory_space_constraint(r, pltpu.VMEM) for r in results])


def solution(mesh):
    split, vector = P("rep", "fsdp", None), P("rep", "fsdp")
    return jax.shard_map(
        local,
        mesh=mesh,
        in_specs=(split, vector, split, split, split, vector, vector, split, P()),
        out_specs=(split, split, split, split, split, vector, vector, vector),
        check_vma=False,
    )
```

```python
import functools

import jax
import jax.numpy as jnp
from jax import lax
from jax.experimental import pallas as pl
from jax.experimental.pallas import tpu as pltpu
from jax.sharding import PartitionSpec as P

STEP = 10
ROUNDS = 4
T = 512
B = 512
D = 4096
KV = 1024
NS = 192
NL = 48
PIECES = ((0, 128), (128, 128), (256, 64), (320, 64), (384, 64), (448, 64))
MESH = pl.DeviceIdType.MESH
F32 = jnp.float32
BF16 = jnp.bfloat16


def adam(param, grad, first, second):
    new_first = 0.9 * first + 0.1 * grad
    new_second = 0.95 * second + 0.05 * grad * grad
    fix_first = 1.0 - 0.9**STEP
    fix_second = 1.0 - 0.95**STEP
    update = new_first / fix_first / (jnp.sqrt(new_second / fix_second) + 1e-08) + 0.1 * param
    return (param - 0.003 * update).astype(BF16), new_first, new_second


def averaged(parts, exponents):
    for e in exponents:
        mixed = []
        for j in range(8):
            partner = jnp.where(e == 0, parts[j ^ 1], jnp.where(e == 1, parts[j ^ 2], parts[j ^ 4]))
            mixed.append(((parts[j] + partner) * 0.5).astype(BF16).astype(F32))
        parts = mixed
    return parts


def packed(row):
    return jnp.concatenate([row[:, 128 * i : 128 * (i + 1)] for i in range(4)] + [jnp.zeros((4, 128), F32)], axis=0)


def unpacked(tile):
    return jnp.concatenate([tile[i : i + 1] for i in range(4)], axis=1)


def kernel(
    x_hbm, gain_ref, w_hbm, m_hbm, v_hbm, gm_ref, gv_ref, cot_hbm, exp_ref,
    vout, xb, wn, m_v, v_v, gout,
    nrm, nt, ntp, wb, cot, cotp, acc, own, held, rstd, slope,
    gb, ggs, ggr, gxs, gxr,
    sd, sr, sl, dr, dl, rr, rl, gs, gr, gt, gf,
    ssem, rsem, lsem,
):
    rep = lax.axis_index("rep")
    f = lax.axis_index("fsdp")
    h, y = f // 4, f % 4
    zlo, rank = rep // 8, rep % 8
    bits = (rank % 2, (rank // 2) % 2, rank // 4)

    def shard(dh, dy):
        return (1 - h if dh else h) * 4 + (y + dy) % 4

    def peer(dh, dy):
        return (rep, shard(dh, dy))

    def mate_rank(j):
        return sum((1 - b if (j >> i) & 1 else b) * (1 << i) for i, b in enumerate(bits))

    def mate(j):
        return (zlo * 8 + mate_rank(j), f)

    right, left, across = peer(0, 1), peer(0, 3), peer(1, 0)

    sent, kept = [], []

    def send(src, dst, device):
        i = len(sent)
        copy = pltpu.make_async_remote_copy(
            src_ref=src, dst_ref=dst, send_sem=ssem.at[i], recv_sem=rsem.at[i],
            device_id=device, device_id_type=MESH,
        )
        copy.start()
        sent.append(copy)
        return copy

    def settle(last):
        while settled[0] < last:
            sent[settled[0]].wait_send()
            settled[0] += 1

    settled = [0]

    def move(src, dst):
        copy = pltpu.make_async_copy(src, dst, lsem.at[len(kept)])
        copy.start()
        kept.append(copy)
        return copy

    def rows(start, size):
        return pl.ds(start, size)

    barrier = pltpu.get_barrier_semaphore()
    others = [peer(i // 4, i % 4) for i in range(1, 8)] + [mate(j) for j in range(1, 8)]
    for device in others:
        pl.semaphore_signal(barrier, inc=1, device_id=device, device_id_type=MESH)
    pl.semaphore_wait(barrier, len(others))

    def back(i):
        return 4 * (i // 4) + (4 - i % 4) % 4

    a1r, a1l, wz = [], [], []
    for k in range(2):
        for pieces, slot, half, device in ((a1r, 3, k, right), (a1l, 1, 1 - k, left)):
            r = rows(256 * half, 256)
            pieces.append(send(w_hbm.at[0, r], wb.at[slot, r], device))
        for q in (2 * k, 2 * k + 1):
            r = rows(128 * q, 128)
            wz.append(send(w_hbm.at[0, r], wb.at[4, r], across))
        if k == 0:
            gb[0] = packed(gain_ref[...].astype(F32))
            gains = [send(gb.at[0], gb.at[back(i)], peer(i // 4, i % 4)) for i in range(1, 8)]
    cot_z = send(cot_hbm.at[0], cotp, across)

    def columns(b):
        return pl.ds(pl.multiple_of(shard(b // 4, b % 4) * B, B), B)

    x_in = [move(x_hbm.at[0, :, columns(b)], xb.at[b]) for b in range(8)]
    cot_in = move(cot_hbm.at[0], cot)
    w_in = move(w_hbm.at[0], wb.at[0])
    m_in = move(m_hbm.at[0], m_v)
    v_in = move(v_hbm.at[0], v_v)
    for copy in x_in:
        copy.wait()

    @pl.loop(0, T // 64)
    def _(i):
        r = pl.ds(pl.multiple_of(i * 64, 64), 64)
        total = jnp.zeros((64, B), F32)
        for b in range(8):
            xf = xb[b, r, :].astype(F32)
            total += xf * xf
        mean = jnp.sum(total, axis=1, keepdims=True) * (1.0 / D)
        rstd[r, :] = jnp.broadcast_to(lax.rsqrt(mean + 1e-05), (64, 128))

    for copy in gains:
        copy.wait_recv()

    def normalise(first, last):
        @pl.loop(first, last)
        def _(b):
            g = unpacked(gb[b])

            @pl.loop(0, T // 128)
            def _(i):
                r = pl.ds(pl.multiple_of(i * 128, 128), 128)
                tile = (xb[b, r, :].astype(F32) * rstd[r, 0:1] * g).astype(BF16)
                nrm[b, r, :] = tile
                nt[b, :, r] = tile.T

    def forward_wz(k):
        wz[k].wait_recv()
        piece = rows(128 * k, 128)
        return (
            send(wb.at[4, piece], wb.at[7, piece], right),
            send(wb.at[4, piece], wb.at[5, piece], left),
        )

    def add_values(b, first=False):
        @pl.loop(0, KV // 256)
        def _(n):
            c = pl.ds(pl.multiple_of(n * 256, 256), 256)
            part = jnp.dot(nrm[b], wb[b, :, c], preferred_element_type=F32)
            acc[:, c] = part if first else acc[:, c] + part

    def send_nt(dy, pair):
        r = rows(256 * pair, 256)
        return send(nt.at[4 + dy, r], ntp.at[dy, r], across)

    a2 = [forward_wz(0)]
    normalise(4, 8)
    a2.append(forward_wz(1))
    nts = {(dy, 0): send_nt(dy, 0) for dy in (2,)}
    for dy, pair in ((2, 1), (1, 0), (3, 0), (0, 0), (1, 1), (3, 1), (0, 1)):
        nts[dy, pair] = send_nt(dy, pair)
    normalise(0, 4)
    w_in.wait()
    a2.append(forward_wz(2))
    add_values(0, True)
    a2.append(forward_wz(3))

    a1r[0].wait_recv()
    a3r = send(wb.at[3, rows(0, 256)], wb.at[2, rows(0, 256)], right)
    a1l[0].wait_recv()
    a3l = send(wb.at[1, rows(256, 256)], wb.at[2, rows(256, 256)], left)
    a1r[1].wait_recv()
    a1l[1].wait_recv()
    add_values(1)
    add_values(3)
    add_values(4)
    for pair in a2:
        pair[0].wait_recv()
        pair[1].wait_recv()
    a4r = send(wb.at[7, rows(0, 192)], wb.at[6, rows(0, 192)], right)
    a4l = send(wb.at[5, rows(320, 192)], wb.at[6, rows(320, 192)], left)
    add_values(5)
    add_values(7)
    cot_in.wait()
    cot_z.wait_recv()

    def gradient(dy, pair, write):
        r = rows(256 * pair, 256)

        @pl.loop(0, KV // 256)
        def _(n):
            c = pl.ds(pl.multiple_of(n * 256, 256), 256)
            part = jnp.dot(nt[dy, r, :], cot[:, c], preferred_element_type=F32)
            part += jnp.dot(ntp[dy, r, :], cotp[:, c], preferred_element_type=F32)
            write(c, part)

    def far_gradient(pair):
        nts[2, pair].wait_recv()

        def write(c, part):
            sd[rows(256 * pair, 256), c] = part.astype(BF16)

        gradient(2, pair, write)

    d2 = {}

    def send_far(pair):
        d2[pair] = []
        for start in (0, 64):
            there = rows(128 * pair + start, 64)
            top, low = rows(256 * pair + start, 64), rows(256 * pair + 128 + start, 64)
            d2[pair].append((send(sd.at[top], dr.at[there], right), send(sd.at[low], dl.at[there], left)))

    far_gradient(0)
    send_far(0)
    far_gradient(1)
    a3r.wait_recv()
    a3l.wait_recv()
    a4z = send(wb.at[2, rows(192, 128)], wb.at[6, rows(192, 128)], across)
    add_values(2)

    def partial_right(pair):
        def write(c, part):
            held[0, :, c] = part[:128]
            sr[rows(256 * pair + 128, 128), c] = part[128:].astype(BF16)

        nts[1, pair].wait_recv()
        gradient(1, pair, write)

    def partial_left(pair):
        def write(c, part):
            sl[rows(256 * pair, 128), c] = part[:128].astype(BF16)
            held[1, :, c] = part[128:]

        nts[3, pair].wait_recv()
        gradient(3, pair, write)

    arriving = {}

    def to_right(start):
        r = rows(start, 64)
        arriving[start].append(send(sr.at[r], rr.at[r], right))

    def to_left(start):
        r = rows(start, 64)
        arriving[start].append(send(sl.at[r], rl.at[r], left))

    def sum_right(pair, k):
        d2[pair][k][0].wait_recv()
        start = 256 * pair + 64 * k
        far = dr[rows(128 * pair + 64 * k, 64), :].astype(F32)
        sr[rows(start, 64), :] = (held[0, rows(64 * k, 64), :] + far).astype(BF16)
        to_right(start)

    def sum_left(pair, k):
        d2[pair][k][1].wait_recv()
        start = 256 * pair + 128 + 64 * k
        far = dl[rows(128 * pair + 64 * k, 64), :].astype(F32)
        sl[rows(start, 64), :] = (held[1, rows(64 * k, 64), :] + far).astype(BF16)
        to_left(start)

    def pass_on(pair, between):
        start = 256 * pair
        for k in range(4):
            arriving[start + 64 * k] = []
        to_left(start)
        to_left(start + 64)
        sum_right(pair, 0)
        sum_left(pair, 0)
        between()
        sum_right(pair, 1)
        to_right(start + 128)
        to_right(start + 192)
        sum_left(pair, 1)

    partial_right(0)
    partial_left(0)
    pass_on(0, lambda: None)
    send_far(1)

    def slopes():
        @pl.loop(0, T // 64)
        def _(i):
            r = pl.ds(pl.multiple_of(i * 64, 64), 64)
            total = acc[r, :]
            vout[r, :] = total.astype(BF16)
            inner = jnp.sum(total * cot[r, :].astype(F32), axis=1, keepdims=True) * (1.0 / D)
            slope[r, :] = inner * rstd[r, :]

    def product(b, n):
        c = pl.ds(n * 256, 256)
        return lax.dot_general(
            cot[...], wb[b, c, :], (((1,), (1,)), ((), ())), preferred_element_type=F32
        )

    def gain_shares(first, last):
        @pl.loop(first, last)
        def _(b):
            for n in range(B // 256):
                xf = xb[b, :, n * 256 : (n + 1) * 256].astype(F32)
                share = jnp.sum(product(b, n) * xf * rstd[:, 0:1], axis=0, keepdims=True)
                for i in range(2):
                    ggs[b, 2 * n + i : 2 * n + i + 1, :] = share[:, 128 * i : 128 * (i + 1)]

    def backward(first, last):
        @pl.loop(first, last)
        def _(b):
            for n in range(B // 256):
                c = pl.ds(n * 256, 256)
                g = unpacked(gb[b])[:, n * 256 : (n + 1) * 256]
                xf = xb[b, :, c].astype(F32)
                xb[b, :, c] = (rstd[:, 0:1] * (product(b, n) * g - xf * slope[:, 0:1])).astype(BF16)

    ggs[...] = jnp.zeros_like(ggs)
    gain_shares(0, 6)
    gain_shares(7, 8)
    gg = [send(ggs.at[i], ggr.at[back(i)], peer(i // 4, i % 4)) for i in (1, 2, 3, 4, 5, 7)]

    exponents = [exp_ref[i] for i in range(ROUNDS)]
    m_in.wait()
    v_in.wait()
    out1, out2 = [], []

    def own_gradient(pair):
        nts[0, pair].wait_recv()

        def write(c, part):
            own[rows(256 * pair, 256), c] = part

        gradient(0, pair, write)

    def step(p):
        r = rows(*PIECES[p])
        for start in range(PIECES[p][0], sum(PIECES[p]), 64):
            for copy in arriving[start]:
                copy.wait_recv()
        for e in range(8):
            c = pl.ds(128 * e, 128)
            grad = own[r, c] + rr[r, c].astype(F32) + rl[r, c].astype(F32)
            stepped, m_v[r, c], v_v[r, c] = adam(wb[0, r, c].astype(F32), grad, m_v[r, c], v_v[r, c])
            gs[e, r, :] = stepped
        out1.append([send(gs.at[mate_rank(j), r], gr.at[j, r], mate(j)) for j in range(1, 8)])

    def mix(p):
        r = rows(*PIECES[p])
        for copy in out1[p]:
            copy.wait_recv()

        start, size = PIECES[p]

        @pl.loop(0, size // 32)
        def _(i):
            q = pl.ds(pl.multiple_of(start + i * 32, 32), 32)
            parts = [gs[rank, q, :].astype(F32)] + [gr[j, q, :].astype(F32) for j in range(1, 8)]
            parts = averaged(parts, exponents)
            for j in range(8):
                gt[j, q, :] = parts[j].astype(BF16)

        out2.append([send(gt.at[j, r], gf.at[rank, r], mate(j)) for j in range(1, 8)])
        gf[rank, r, :] = gt[0, r, :]

    def finish(p):
        r = rows(*PIECES[p])
        for copy in out2[p]:
            copy.wait_recv()
        for e in range(8):
            wn[r, 128 * e : 128 * (e + 1)] = gf[e, r, :]

    own_gradient(0)
    step(0)
    partial_right(1)
    step(1)
    partial_left(1)
    early = len(sent)
    pass_on(1, lambda: mix(0))
    ready = len(sent)
    own_gradient(1)
    mix(1)
    settle(early)
    step(2)
    step(3)
    for copy in (a4r, a4l, a4z):
        copy.wait_recv()
    add_values(6)
    gain_shares(6, 7)
    gg.append(send(ggs.at[6], ggr.at[back(6)], peer(1, 2)))
    step(4)
    step(5)
    slopes()

    mix(2)
    mix(3)

    for copy in gg:
        copy.wait_recv()
    total = ggs[0]
    for i in range(1, 8):
        total += ggr[i]
    stepped, first, second = adam(gain_ref[...].astype(F32), unpacked(total), gm_ref[...], gv_ref[...])
    gout[1:2, :] = first
    gout[2:3, :] = second
    gxs[...] = packed(stepped.astype(F32))
    gx = [send(gxs, gxr.at[j], mate(j)) for j in range(1, 8)]

    backward(0, 2)
    mix(4)
    mix(5)
    for p in range(2):
        finish(p)
    backward(2, 8)
    for copy in gx:
        copy.wait_recv()
    parts = averaged([gxs[...]] + [gxr[j] for j in range(1, 8)], exponents)
    gout[0:1, :] = unpacked(parts[0])
    settle(len(sent) - 28)
    for p in range(2, len(PIECES)):
        finish(p)

    settle(len(sent))


def write_out(vout, xb, wn, m_v, v_v, gout, val, ig, nw, nm, nv, ng, ngm, ngv, sem):
    f = lax.axis_index("fsdp")
    h, y = f // 4, f % 4
    pairs = [(vout, val.at[0]), (wn, nw.at[0]), (m_v, nm.at[0]), (v_v, nv.at[0])]
    for b in range(8):
        column = ((1 - h if b // 4 else h) * 4 + (y + b % 4) % 4) * B
        pairs.append((xb.at[b], ig.at[0, :, pl.ds(pl.multiple_of(column, B), B)]))
    copies = [pltpu.make_async_copy(src, dst, sem.at[i]) for i, (src, dst) in enumerate(pairs)]
    for copy in copies:
        copy.start()
    ng[...] = gout[0:1, :].astype(BF16)
    ngm[...] = gout[1:2, :]
    ngv[...] = gout[2:3, :]
    for copy in copies:
        copy.wait()


def local(*args):
    any_space, vmem = pl.BlockSpec(memory_space=pl.ANY), pl.BlockSpec(memory_space=pltpu.VMEM)
    smem = pl.BlockSpec(memory_space=pltpu.SMEM)
    shapes = [
        ((1, T, KV), BF16), ((1, T, D), BF16), ((1, B, KV), BF16), ((1, B, KV), F32), ((1, B, KV), F32),
        ((1, B), BF16), ((1, B), F32), ((1, B), F32),
    ]
    held = [
        ((T, KV), BF16), ((8, T, B), BF16), ((B, KV), BF16), ((B, KV), F32), ((B, KV), F32), ((8, B), F32),
    ]
    scratch = [
        ((8, T, B), BF16), ((8, B, T), BF16), ((4, B, T), BF16),
        ((8, B, KV), BF16), ((T, KV), BF16), ((T, KV), BF16),
        ((T, KV), F32), ((B, KV), F32), ((2, 128, KV), F32), ((T, 128), F32), ((T, 128), F32),
        ((8, 8, 128), F32), ((8, 8, 128), F32), ((8, 8, 128), F32), ((8, 128), F32), ((8, 8, 128), F32),
        ((B, KV), BF16), ((B, KV), BF16), ((B, KV), BF16), ((B // 2, KV), BF16), ((B // 2, KV), BF16),
        ((B, KV), BF16), ((B, KV), BF16),
        ((8, B, 128), BF16), ((8, B, 128), BF16), ((8, B, 128), BF16), ((8, B, 128), BF16),
    ]
    results = pl.pallas_call(
        kernel,
        out_shape=[pltpu.VMEM(s, t) for s, t in held],
        in_specs=[any_space, vmem, any_space, any_space, any_space, vmem, vmem, any_space, smem],
        out_specs=[vmem] * len(held),
        scratch_shapes=[pltpu.VMEM(s, t) for s, t in scratch]
        + [pltpu.SemaphoreType.DMA((NS,)), pltpu.SemaphoreType.DMA((NS,)), pltpu.SemaphoreType.DMA((NL,))],
        compiler_params=pltpu.CompilerParams(
            collective_id=0, has_side_effects=True, vmem_limit_bytes=46 << 20
        ),
        cost_estimate=pl.CostEstimate(flops=6 * T * D * KV, bytes_accessed=20 << 20, transcendentals=0),
        name="layer_step",
    )(*args)
    return pl.pallas_call(
        write_out,
        out_shape=[jax.ShapeDtypeStruct(s, t) for s, t in shapes],
        in_specs=[vmem] * len(held),
        out_specs=[any_space] * 5 + [vmem] * 3,
        scratch_shapes=[pltpu.SemaphoreType.DMA((12,))],
        compiler_params=pltpu.CompilerParams(vmem_limit_bytes=4 << 20),
        name="write_out",
    )(*[pltpu.with_memory_space_constraint(r, pltpu.VMEM) for r in results])


def solution(mesh):
    split, vector = P("rep", "fsdp", None), P("rep", "fsdp")
    return jax.shard_map(
        local,
        mesh=mesh,
        in_specs=(split, vector, split, split, split, vector, vector, split, P()),
        out_specs=(split, split, split, split, split, vector, vector, vector),
        check_vma=False,
    )
```
